256 devices in a mesh: ctx: 32 (over x, z_lo, core), exp: 8 (over y, z_hi).
Axes of the slice: x: 4, y: 4, z: 8 (z_hi: 2, z_lo: 4; z = z_hi * 4 + z_lo), core: 2. Of those that a mesh axis runs over, the one named last changes fastest.
Arguments:
- queries: bfloat16 [2048, 6144], P('ctx', 'exp'), may hold values from -120 to 120
- rotated_key_cache: bfloat16 [8192, 1024], P('ctx', 'exp'), may hold values from -4.1 to 4.1
- value_cache_rows: bfloat16 [8192, 1024], P('ctx', 'exp'), may hold values from -6 to 6
- kv_pos: int32 [8192], P('ctx'), may hold values from 0 to 8191, as said below
- q_pos: int32 [2048], P('ctx'), may hold values from 4096 to 8191
- residual: bfloat16 [2048, 6144], P('exp', 'ctx'), may hold values from -30 to 30
- w_out: bfloat16 [6144, 6144], P('exp', 'ctx'), may hold values from -0.078125 to 0.078125
- norm_gain: bfloat16 [6144], P('ctx'), may hold values from 0.099609375 to 1.8984375
- routes: int32 [2048, 2], P('exp'), may hold values from 0 to 7, all different within a row; in each aligned block of 256 rows (0 to 255, 256 to 511, ...) at most 192 rows name the same one
- gate_probs: float32 [2048, 2], P('exp'), may hold values from 0.1 to 1
- w_gate: bfloat16 [8, 6144, 8192], P('exp', None, 'ctx'), may hold values from -0.078125 to 0.078125
- w_up: bfloat16 [8, 6144, 8192], P('exp', None, 'ctx'), may hold values from -0.078125 to 0.078125
- w_down: bfloat16 [8, 8192, 6144], P('exp', 'ctx'), may hold values from -0.0625 to 0.0625
Outputs:
- attended: bfloat16 [2048, 6144], P('ctx', 'exp')
- mixed: bfloat16 [2048, 6144], P('exp', 'ctx')
The draws below stay inside these ranges and needn't reach their ends.
Inputs may be any that keep to these rules, and one draw needn't show every extreme that they name: `routes`: in each aligned block of 256 rows (the tokens of one index of exp) no expert is named by more than 192 rows; the two experts of a row differ. `kv_pos`: each position 0 to 8191 appears once; each aligned run of 128 slots holds consecutive positions in increasing order.
All inputs are finite; a program needn't handle non-finite values.
Results may differ from the reference program's by a relative error of at most 0.015.
Values may be sent and summed in bfloat16 or wider, within the bound.
A program may use at most 128 MiB of HBM per device.

```python
import math
import jax
import jax.numpy as jnp
import numpy as np
from jax import lax

D = 6144
HEAD_SIZE = 128
QUERY_PER_GROUP = 6
FF = 8192
TOP = 2
PAGE = 128
SLAB_TOKENS = 64
QUERY_HEADS = 48
KEY_VALUE_HEADS = 8
EXPERTS = 8
SLAB = 2048
CACHE_POSITIONS = 8192
TOKX = 256
CAP = 192
N_CTX = 32
N_EXP = 8


def page_order(key):
    return jax.random.permutation(jax.random.fold_in(key, 11), CACHE_POSITIONS // PAGE)


def base_keys(key):
    return jnp.clip(jax.random.normal(jax.random.fold_in(key, 12), (CACHE_POSITIONS, KEY_VALUE_HEADS * HEAD_SIZE), jnp.float32), -4.0, 4.0)


def draw_kv_pos(key, part):
    order = page_order(key)
    slots = order[:, None] * PAGE + jnp.arange(PAGE, dtype=jnp.int32)[None, :]
    return slots.reshape(CACHE_POSITIONS).astype(jnp.int32)


def draw_rotated_key_cache(key, part):
    values_drawn = base_keys(key)
    return values_drawn.astype(jnp.bfloat16)


def draw_queries(key, part):
    key = jax.random.fold_in(key, 5)
    drawn = jnp.clip(jax.random.normal(key, (SLAB, QUERY_HEADS * HEAD_SIZE), jnp.float32) * 3.0, -15.0, 15.0)
    return drawn.astype(jnp.bfloat16)


def draw_residual(key, part):
    key = jax.random.fold_in(key, 6)
    columns = jnp.arange(D).astype(jnp.float32)
    col_scale = 0.5 * jnp.exp(jnp.log(3.0) * columns / (D - 1))
    drawn = jnp.clip(jax.random.normal(key, (SLAB, D), jnp.float32), -6.0, 6.0) * col_scale[None, :]
    return drawn.astype(jnp.bfloat16)


def plant(values, rng, smallest, largest):
    spot = [jax.random.randint(jax.random.fold_in(rng, axis), (), 0, length) for axis, length in enumerate(values.shape)]
    widest = values.shape.index(max(values.shape))
    neighbour = spot[:widest] + [(spot[widest] + 1) % values.shape[widest]] + spot[widest + 1:]
    return values.at[tuple(spot)].set(smallest).at[tuple(neighbour)].set(largest)


def shard_levels(rng, extent, pieces, low, largest):
    level, own = 1.0, jax.random.fold_in(rng, 6)
    for axis_at, shards_of in pieces:
        heights = jnp.exp(jax.random.uniform(jax.random.fold_in(own, axis_at), (shards_of,), jnp.float32, low / len(pieces), largest / len(pieces)))
        level = level * jnp.repeat(heights, extent[axis_at] // shards_of).reshape([-1 if axis == axis_at else 1 for axis in range(len(extent))])
    return level


def deal_out(rng, own, number, rows, amount, top, reach, slope):
    sequence = jax.random.permutation(rng, amount)
    packed, ordinary = shares(amount, rows * top, reach, slope, True), shares(amount, rows * top, reach, slope, False)
    places = jnp.arange(amount)

    def named(sizes, rotation):
        used = int((sizes > 0).sum())
        fixed = max(1, used // 4)
        moved = fixed + (places - fixed + rotation * (used - fixed)) % max(1, amount - fixed)
        return jnp.zeros((amount,), jnp.int32).at[sequence[jnp.where(places < fixed, places, moved)]].set(jnp.asarray(sizes, jnp.int32))

    sizes = jnp.where(number % 4 == 0, named(packed, number // 4), named(ordinary, number - number // 4 - 1))
    mixed = jax.random.permutation(jax.random.fold_in(own, 3), amount)
    source_of, receiver = mixed[0:amount // 2 * 2:2], mixed[1:amount // 2 * 2:2]
    slack = jnp.minimum(sizes[source_of] - 1, reach - sizes[receiver]) // 2
    slack = jnp.where((source_of == sequence[0]) | (receiver == sequence[0]) | (sizes[receiver] == 0), 0, jnp.maximum(slack, 0))
    moved = jax.random.randint(jax.random.fold_in(own, 4), (amount // 2,), 0, 1 << 20) % (slack + 1)
    sizes = sizes.at[source_of].add(-moved).at[receiver].add(moved)
    members = jnp.searchsorted(jnp.cumsum(sizes), jnp.arange(rows * top), side="right").astype(jnp.int32)
    listing = members.reshape(top, rows).T
    listing = listing[jax.random.permutation(jax.random.fold_in(own, 1), rows)]
    rotation = jax.random.randint(jax.random.fold_in(own, 2), (rows, 1), 0, top)
    return jnp.take_along_axis(listing, (jnp.arange(top)[None, :] + rotation) % top, axis=1)


def shares(count, total, reach, slope, full):
    loads = [(1 << 20) // math.isqrt(grade ** slope) + 1 for grade in range(1, count + 1)]
    largest = reach if full else min(reach, max(-(-total // count), total * loads[0] // sum(loads)))
    least = 1 if total - largest >= count - 1 else 0
    holding, surplus = [largest] + [least] * (count - 1), total - largest - least * (count - 1)
    while surplus > 0:
        movable = [i for i in range(1, count) if holding[i] < largest] or [i for i in range(1, count) if holding[i] < reach]
        whole, left = sum([loads[i] for i in movable]), surplus
        for i in movable:
            addition = min(reach - holding[i], max(1, left * loads[i] // whole), surplus)
            holding[i] = holding[i] + addition
            surplus = surplus - addition
    return np.array(holding)


def normal_values(key, extent, width, bound, cuts=(), kind=jnp.bfloat16):
    loudness = shard_levels(key, extent, cuts, -0.22, 0.18) if cuts else 1.0
    array = jax.random.normal(key, extent, jnp.float32) * width * loudness
    return jnp.minimum(jnp.maximum(array, -bound), bound).astype(kind)


def setup_inputs(seed: int = 0) -> dict:
    seeds = jax.random.split(jax.random.key(seed), 14)
    queries = draw_queries(jax.random.fold_in(seeds[13], 71), 0)
    rotated_key_cache = draw_rotated_key_cache(jax.random.fold_in(seeds[13], 71), 0)
    value_cache_rows = normal_values(seeds[2], (CACHE_POSITIONS, KEY_VALUE_HEADS * HEAD_SIZE), 1.0, 6.0, ((0, 32), (1, 8)))
    kv_pos = draw_kv_pos(jax.random.fold_in(seeds[13], 71), 0)
    q_pos = plant(jax.random.randint(seeds[4], (SLAB,), CACHE_POSITIONS // 2, CACHE_POSITIONS), jax.random.fold_in(seeds[4], 1), CACHE_POSITIONS // 2, CACHE_POSITIONS - 1).astype(jnp.int32)
    residual = draw_residual(jax.random.fold_in(seeds[13], 71), 0)
    w_out = normal_values(seeds[6], (QUERY_HEADS * HEAD_SIZE, D), (QUERY_HEADS * HEAD_SIZE) ** -0.5, 0.078125, ((0, 8), (1, 32)))
    norm_gain = jnp.clip(1.0 + 0.18 * jax.random.normal(seeds[7], (D,), jnp.float32), 0.099609375, 1.8984375).astype(jnp.bfloat16)
    routes_keys = jax.random.split(jax.random.fold_in(seeds[8], 1), SLAB // TOKX)
    routes_turns = jax.random.permutation(jax.random.fold_in(seeds[8], 3), SLAB // TOKX)
    routes = jax.vmap(lambda own, number: deal_out(jax.random.fold_in(seeds[8], 2), own, number, TOKX, EXPERTS, TOP, CAP, 2))(routes_keys, routes_turns).reshape((SLAB, TOP))
    gate_probs = jnp.clip(jnp.exp(math.log(1.0) - 2.3025851 * jax.random.uniform(seeds[9], (SLAB, TOP), jnp.float32) ** shard_levels(seeds[9], (SLAB, TOP), ((0, 8),), -0.2, 0.2)), 0.1, 1.0)
    w_gate = normal_values(seeds[10], (EXPERTS, D, FF), D ** -0.5, 0.078125, ((0, 8), (2, 32)))
    w_up = normal_values(seeds[11], (EXPERTS, D, FF), D ** -0.5, 0.078125, ((0, 8), (2, 32)))
    w_down = normal_values(seeds[12], (EXPERTS, FF, D), FF ** -0.5, 0.0625, ((0, 8), (1, 32)))
    return {"queries": queries, "rotated_key_cache": rotated_key_cache, "value_cache_rows": value_cache_rows, "kv_pos": kv_pos, "q_pos": q_pos, "residual": residual, "w_out": w_out, "norm_gain": norm_gain, "routes": routes, "gate_probs": gate_probs, "w_gate": w_gate, "w_up": w_up, "w_down": w_down}


neg_big = -1e+30
epsilon = 1e-05

def head_block(q_block, pos_block, key_head, value_head, kv_pos):
    scores = jnp.einsum('tqd,kd->tqk', q_block.astype(jnp.float32), key_head.astype(jnp.float32), precision=lax.Precision.HIGHEST) * HEAD_SIZE ** (-0.5)
    allowed = kv_pos[None, None, :] <= pos_block[:, None, None]
    scores = jnp.where(allowed, scores, neg_big)
    highest = lax.optimization_barrier(jnp.max(scores, axis=2, keepdims=True))
    weights = jnp.where(allowed, jnp.exp(scores - highest), 0.0)
    totals = lax.optimization_barrier(jnp.sum(weights, axis=2, keepdims=True))
    blended = jnp.einsum('tqk,kd->tqd', weights, value_head.astype(jnp.float32), precision=lax.Precision.HIGHEST)
    return (blended / totals).astype(jnp.bfloat16)

def attention(queries, rotated_key_cache, value_cache_rows, kv_pos, q_pos):
    block_list = SLAB // SLAB_TOKENS
    query_head_split = queries.reshape(block_list, SLAB_TOKENS, KEY_VALUE_HEADS, QUERY_PER_GROUP, HEAD_SIZE).transpose(2, 0, 1, 3, 4)
    pos_blocks = q_pos.reshape(block_list, SLAB_TOKENS)
    key_head_split = rotated_key_cache.reshape(CACHE_POSITIONS, KEY_VALUE_HEADS, HEAD_SIZE).transpose(1, 0, 2)
    value_head_split = value_cache_rows.reshape(CACHE_POSITIONS, KEY_VALUE_HEADS, HEAD_SIZE).transpose(1, 0, 2)

    def per_head(inputs):
        q_head, key_head, value_head = inputs

        def per_block(inner):
            return head_block(inner[0], inner[1], key_head, value_head, kv_pos)
        return lax.map(per_block, (q_head, pos_blocks))
    result = lax.map(per_head, (query_head_split, key_head_split, value_head_split))
    return result.transpose(1, 2, 0, 3, 4).reshape(SLAB, QUERY_HEADS * HEAD_SIZE)

def experts_mix(normed, routes, gate_probs, w_gate, w_up, w_down):
    flat_ids = routes.reshape(-1)
    flat_probs = gate_probs.reshape(-1).astype(jnp.float32)
    limit = N_EXP * CAP

    def add_expert(expert, total):
        order = jnp.argsort((flat_ids != expert).astype(jnp.int32), stable=True)[:limit]
        valid = flat_ids[order] == expert
        token = (order // TOP).astype(jnp.int32)
        rows = normed[token]
        gate_mat = lax.dynamic_index_in_dim(w_gate, expert, 0, keepdims=False)
        up_mat = lax.dynamic_index_in_dim(w_up, expert, 0, keepdims=False)
        down_mat = lax.dynamic_index_in_dim(w_down, expert, 0, keepdims=False)
        gate_val = jnp.dot(rows, gate_mat, preferred_element_type=jnp.float32)
        up_val = jnp.dot(rows, up_mat, preferred_element_type=jnp.float32)
        active = (jax.nn.silu(gate_val) * up_val).astype(jnp.bfloat16)
        act_blocks = active.reshape(limit, N_CTX, FF // N_CTX).transpose(1, 0, 2)
        down_blocks = down_mat.reshape(N_CTX, FF // N_CTX, D)

        def add_block(accum, pair):
            portion = jnp.dot(pair[0], pair[1], preferred_element_type=jnp.float32).astype(jnp.bfloat16)
            portion = lax.optimization_barrier(portion)
            return (accum + portion.astype(jnp.float32), None)
        summed, _ = lax.scan(add_block, jnp.zeros((limit, D), jnp.float32), (act_blocks, down_blocks))
        rounded = lax.optimization_barrier(summed.astype(jnp.bfloat16))
        scaled = jnp.where(valid[:, None], flat_probs[order][:, None] * rounded.astype(jnp.float32), 0.0)
        return total.at[token].add(scaled)
    return lax.fori_loop(0, EXPERTS, add_expert, jnp.zeros((SLAB, D), jnp.float32))

def reference(queries, rotated_key_cache, value_cache_rows, kv_pos, q_pos, residual, w_out, norm_gain, routes, gate_probs, w_gate, w_up, w_down):
    attended = attention(queries, rotated_key_cache, value_cache_rows, kv_pos, q_pos)
    attn_out = jnp.dot(attended, w_out, preferred_element_type=jnp.float32)
    stream = residual.astype(jnp.float32) + attn_out
    inverse = lax.rsqrt(lax.optimization_barrier(jnp.mean(stream * stream, axis=1, keepdims=True)) + epsilon)
    normed = (stream * inverse * norm_gain.astype(jnp.float32)[None, :]).astype(jnp.bfloat16)
    mixture = experts_mix(normed, routes, gate_probs, w_gate, w_up, w_down)
    mixed = (stream + mixture).astype(jnp.bfloat16)
    return (attended, mixed)
```

```python
import functools

import jax
import jax.numpy as jnp
from jax import lax
from jax.experimental import pallas as pl
from jax.experimental.pallas import tpu as pltpu
from jax.sharding import Mesh
from jax.sharding import PartitionSpec as P

MESH = pl.DeviceIdType.MESH
DMA = pltpu.SemaphoreType.DMA
D = 6144
NX, NZ = 4, 4
neg_big = -1e30
epsilon = 1e-05


def remote(src, dst, send_sem, recv_sem, device):
    return pltpu.make_async_remote_copy(
        src_ref=src,
        dst_ref=dst,
        send_sem=send_sem,
        recv_sem=recv_sem,
        device_id=device,
        device_id_type=MESH,
    )


def enter(devices):
    barrier = pltpu.get_barrier_semaphore()
    for device in devices:
        pl.semaphore_signal(barrier, inc=1, device_id=device, device_id_type=MESH)
    pl.semaphore_wait(barrier, len(devices))


def plane_peers(x, z):
    peers = [{"x": lax.rem(x + 1, NX)}, {"x": lax.rem(x + 3, NX)}]
    return peers + [{"z": lax.rem(z + step, NZ)} for step in range(1, NZ)]


def gather_kernel(share, cut, in_ref, out_ref, own_sem, zs, zr, xs, xr, fs, fr, ks, kr, hs, hr):
    x, z, k = lax.axis_index("x"), lax.axis_index("z"), lax.axis_index("k")
    up, down, across = lax.rem(x + 1, NX), lax.rem(x + 3, NX), lax.rem(x + 2, NX)
    rows = in_ref.shape[0]
    halves = ((0, cut), (cut, rows - cut))
    width = 2 if share else 1

    def spot(bx, bz, core, half=None):
        where = (bx * NZ + bz) * width + (core if share else 0)
        if half is None:
            return out_ref.at[where]
        return out_ref.at[where, pl.ds(*halves[half])]

    enter(plane_peers(x, z) + ([{"k": 1 - k}] if share else []))
    sent = []

    def send(src, dst, send_sem, recv_sem, device):
        copy = remote(src, dst, send_sem, recv_sem, device)
        copy.start()
        sent.append(copy)

    def arrived(ref, send_sem, recv_sem):
        remote(ref, ref, send_sem, recv_sem, {"x": up}).wait_recv()

    own = pltpu.make_async_copy(in_ref, spot(x, z, k), own_sem)
    own.start()
    for step in range(1, NZ):
        send(in_ref, spot(x, z, k), zs.at[step - 1], zr.at[step - 1], {"z": lax.rem(z + step, NZ)})
    for step in range(NZ):
        bz = lax.rem(z + NZ - step, NZ)
        dst = spot(x, bz, k)
        src = in_ref if step == 0 else dst
        if step:
            arrived(dst, zs.at[step - 1], zr.at[step - 1])
        send(src, dst, xs.at[0, step], xr.at[0, step], {"x": up})
        send(src, dst, xs.at[1, step], xr.at[1, step], {"x": down})
        if share:
            send(src, dst, ks.at[0, step], kr.at[0, step], {"k": 1 - k})
    for step in range(NZ):
        bz = lax.rem(z + NZ - step, NZ)
        for way, (came, goes) in enumerate(((down, up), (up, down))):
            block = spot(came, bz, k)
            arrived(block, xs.at[way, step], xr.at[way, step])
            half = spot(came, bz, k, way)
            send(half, half, fs.at[way, step], fr.at[way, step], {"x": goes})
            if share:
                send(block, block, ks.at[1 + way, step], kr.at[1 + way, step], {"k": 1 - k})
    for step in range(NZ):
        bz = lax.rem(z + NZ - step, NZ)
        for way in range(2):
            half = spot(across, bz, k, way)
            arrived(half, fs.at[way, step], fr.at[way, step])
            if share:
                send(half, half, hs.at[way, step], hr.at[way, step], {"k": 1 - k})
    if share:
        for step in range(NZ):
            bz = lax.rem(z + NZ - step, NZ)
            for which, bx in enumerate((x, down, up)):
                arrived(spot(bx, bz, 1 - k), ks.at[which, step], kr.at[which, step])
            for way in range(2):
                arrived(spot(across, bz, 1 - k, way), hs.at[way, step], hr.at[way, step])
    for copy in sent:
        copy.wait_send()
    own.wait()


def plane_gather(block, collective_id, share=False, cut=None):
    rows = block.shape[0]
    count = NX * NZ * (2 if share else 1)
    return pl.pallas_call(
        functools.partial(gather_kernel, share, rows // 2 if cut is None else cut),
        out_shape=jax.ShapeDtypeStruct((count,) + block.shape, block.dtype),
        in_specs=[pl.BlockSpec(memory_space=pl.ANY)],
        out_specs=pl.BlockSpec(memory_space=pl.ANY),
        scratch_shapes=[
            DMA,
            DMA((3,)),
            DMA((3,)),
            DMA((2, 4)),
            DMA((2, 4)),
            DMA((2, 4)),
            DMA((2, 4)),
            DMA((3, 4)),
            DMA((3, 4)),
            DMA((2, 4)),
            DMA((2, 4)),
        ],
        compiler_params=pltpu.CompilerParams(
            collective_id=collective_id, has_side_effects=True, vmem_limit_bytes=16 << 20
        ),
        name=f"plane_gather_{collective_id}",
    )(block)


def scatter_kernel(
    part_ref, out_ref, relay, from_x, mine, from_z, rs, rr, xs, xr, us, ur, zs, zr
):
    x, z = lax.axis_index("x"), lax.axis_index("z")
    up, down, across = lax.rem(x + 1, NX), lax.rem(x + 3, NX), lax.rem(x + 2, NX)
    width = out_ref.shape[1]
    half = out_ref.shape[0] // 2
    tile = 48

    def part(bx, bz, which=None):
        at = pl.ds(pl.multiple_of((bx * NZ + bz) * width, 128), width)
        if which is None:
            return part_ref.at[:, at]
        return part_ref.at[pl.ds(which * half, half), at]

    enter(plane_peers(x, z))
    sent = []

    def send(src, dst, send_sem, recv_sem, device):
        copy = remote(src, dst, send_sem, recv_sem, device)
        copy.start()
        sent.append(copy)

    def arrived(ref, send_sem, recv_sem):
        remote(ref, ref, send_sem, recv_sem, {"x": up}).wait_recv()

    def add(dst, terms, rows):
        @pl.loop(0, rows // tile)
        def _(i):
            at = pl.ds(i * tile, tile)
            total = terms[0][at, :].astype(jnp.float32)
            for term in terms[1:]:
                total = total + term[at, :].astype(jnp.float32)
            dst[at, :] = total.astype(dst.dtype)

    ways = (up, down)
    order = [lax.rem(z + step, NZ) for step in (1, 2, 3, 0)]
    for step in range(NZ):
        bz = order[step]
        for way, goes in enumerate(ways):
            send(part(across, bz, way), relay.at[way, step], rs.at[way, step], rr.at[way, step], {"x": goes})
    for step in range(NZ):
        bz = order[step]
        for way, goes in enumerate(ways):
            other = 1 - way
            send(
                part(goes, bz, other),
                from_x.at[way, step, pl.ds(other * half, half)],
                us.at[way, step],
                ur.at[way, step],
                {"x": goes},
            )
    for step in range(NZ):
        bz = order[step]
        for way, goes in enumerate(ways):
            held = relay.at[way, step]
            arrived(held, rs.at[way, step], rr.at[way, step])
            add(held, (held, part(goes, bz, way)), half)
            send(
                held,
                from_x.at[way, step, pl.ds(way * half, half)],
                xs.at[way, step],
                xr.at[way, step],
                {"x": goes},
            )
    for step in range(NZ):
        bz = order[step]
        for way in range(2):
            held = from_x.at[way, step]
            arrived(held.at[pl.ds(way * half, half)], xs.at[way, step], xr.at[way, step])
            arrived(held.at[pl.ds((1 - way) * half, half)], us.at[way, step], ur.at[way, step])
        add(mine.at[step], (part(x, bz), from_x.at[0, step], from_x.at[1, step]), 2 * half)
        if step < NZ - 1:
            send(mine.at[step], from_z.at[step], zs.at[step], zr.at[step], {"z": bz})
    for step in range(NZ - 1):
        arrived(from_z.at[step], zs.at[step], zr.at[step])
    add(out_ref, (mine.at[NZ - 1], from_z.at[0], from_z.at[1], from_z.at[2]), 2 * half)
    for copy in sent:
        copy.wait_send()


def plane_scatter(partial, collective_id):
    rows, width = partial.shape[0], partial.shape[1] // (NX * NZ)
    kind = partial.dtype
    return pl.pallas_call(
        scatter_kernel,
        out_shape=jax.ShapeDtypeStruct((rows, width), kind),
        in_specs=[pl.BlockSpec(memory_space=pltpu.VMEM)],
        out_specs=pl.BlockSpec(memory_space=pltpu.VMEM),
        scratch_shapes=[
            pltpu.VMEM((2, NZ, rows // 2, width), kind),
            pltpu.VMEM((2, NZ, rows, width), kind),
            pltpu.VMEM((NZ, rows, width), kind),
            pltpu.VMEM((NZ - 1, rows, width), kind),
        ]
        + [DMA((2, 4))] * 6
        + [DMA((3,))] * 2,
        compiler_params=pltpu.CompilerParams(
            collective_id=collective_id, has_side_effects=True, vmem_limit_bytes=48 << 20
        ),
        name=f"plane_scatter_{collective_id}",
    )(partial)


def swap(array):
    return lax.ppermute(array, "k", [(0, 1), (1, 0)])


def beside(own, other, k, axis):
    return jnp.where(
        k == 0,
        jnp.concatenate([own, other], axis=axis),
        jnp.concatenate([other, own], axis=axis),
    )


def local(
    queries,
    rotated_key_cache,
    value_cache_rows,
    kv_pos,
    q_pos,
    residual,
    w_out,
    norm_gain,
    routes,
    gate_probs,
    w_gate,
    w_up,
    w_down,
):
    k = lax.axis_index("k")
    chip = lax.axis_index("x") * NZ + lax.axis_index("z")
    tokens, head_dim = queries.shape[0], rotated_key_cache.shape[1]
    heads = queries.shape[1] // head_dim
    feats = residual.shape[1]
    block_tokens = residual.shape[0]

    wg, wu, wd = w_gate[0], w_up[0], w_down[0]
    wg2, wu2, wd2 = swap(wg), swap(wu), swap(wd)
    w_out2 = beside(w_out, swap(w_out), k, 1)
    by_core = residual.reshape(2, 2, tokens, feats)
    res_own = lax.dynamic_index_in_dim(by_core, k, 1, keepdims=False).reshape(2 * tokens, feats)
    res_give = lax.dynamic_index_in_dim(by_core, 1 - k, 1, keepdims=False).reshape(2 * tokens, feats)
    res = beside(res_own, swap(res_give), k, 1)

    pages = (kv_pos.reshape(2, 128)[:, 0] // 128).astype(jnp.bfloat16)
    extra = jnp.zeros((16, 2 * head_dim), jnp.bfloat16)
    extra = extra.at[0, :2].set(pages).at[1, :feats].set(norm_gain)
    block = jnp.concatenate(
        [jnp.concatenate([rotated_key_cache, value_cache_rows], axis=1), extra], axis=0
    )
    gathered = plane_gather(block, 1, share=True, cut=144)
    keys = gathered[:, :256, :head_dim].reshape(-1, head_dim)
    values = gathered[:, :256, head_dim:].reshape(-1, head_dim)
    starts = gathered[:, 256, :2].astype(jnp.int32) * 128
    positions = (starts.reshape(-1, 1) + jnp.arange(128, dtype=jnp.int32)[None, :]).reshape(-1)
    gains = gathered[:, 257, :feats].astype(jnp.float32).reshape(-1)

    rows = queries.reshape(tokens * heads, head_dim)
    row_pos = jnp.repeat(q_pos, heads)
    scores = lax.dot_general(
        rows, keys, (((1,), (1,)), ((), ())), preferred_element_type=jnp.float32
    ) * (head_dim**-0.5)
    scores = jnp.where(positions[None, :] <= row_pos[:, None], scores, neg_big)
    weights = jnp.exp(scores - jnp.max(scores, axis=1, keepdims=True))
    totals = jnp.sum(weights, axis=1, keepdims=True)
    blended = jnp.dot(weights.astype(jnp.bfloat16), values, preferred_element_type=jnp.float32)
    attended = (blended / totals).reshape(tokens, heads * head_dim).astype(jnp.bfloat16)

    slab = plane_gather(attended, 2).reshape(NX * NZ * tokens, heads * head_dim)
    projected = jnp.dot(slab, w_out2, preferred_element_type=jnp.float32).astype(jnp.bfloat16)
    pieces = lax.all_to_all(
        projected.reshape(8, 2 * tokens, 2 * feats), ("y", "w"), 0, 0, tiled=True
    )
    stream = res.astype(jnp.float32) + jnp.sum(pieces.astype(jnp.float32), axis=0)

    own_gain = lax.dynamic_slice_in_dim(gains, chip * 2 * feats, 2 * feats)
    scaled = (stream * own_gain[None, :]).astype(jnp.bfloat16)
    both = beside(
        scaled.reshape(2, 1, tokens, 2 * feats), swap(scaled).reshape(2, 1, tokens, 2 * feats), k, 1
    ).reshape(block_tokens, 2 * feats)

    experts, choices = 8, routes.shape[1]
    slots = 6 * block_tokens // experts // 2
    flat_ids = routes.reshape(-1)
    onehot = (flat_ids[:, None] == jnp.arange(experts, dtype=jnp.int32)[None, :]).astype(jnp.int32)
    earlier = jnp.cumsum(onehot, axis=0) - onehot
    slot = jnp.sum(earlier * onehot, axis=1) - k * slots
    cell = jnp.where((slot >= 0) & (slot < slots), flat_ids * slots + slot, -1)
    layout = cell[:, None] == jnp.arange(experts * slots, dtype=jnp.int32)[None, :]
    layout = layout.reshape(block_tokens, choices, experts * slots)
    placer = jnp.any(layout, axis=1).astype(jnp.bfloat16)
    picker = jnp.sum(jnp.where(layout, gate_probs[:, :, None], 0.0), axis=1)
    picker_high = picker.astype(jnp.bfloat16)
    picker_low = (picker - picker_high.astype(jnp.float32)).astype(jnp.bfloat16)

    outgoing = lax.dot_general(
        placer, both, (((0,), (0,)), ((), ())), preferred_element_type=jnp.float32
    ).astype(jnp.bfloat16)
    arrived = lax.all_to_all(
        outgoing.reshape(experts, slots, 2 * feats), ("y", "w"), 0, 0, tiled=True
    )
    spread = plane_gather(arrived.reshape(experts * slots, 2 * feats), 3)
    inner = spread.transpose(1, 0, 2).reshape(experts * slots, D)
    wide = inner.astype(jnp.float32)
    squares = jnp.sum(wide * wide * (1.0 / (gains * gains))[None, :], axis=1, keepdims=True)
    inverse = lax.rsqrt(squares / D + epsilon)

    def hidden(gate_mat, up_mat):
        gate_val = jnp.dot(inner, gate_mat, preferred_element_type=jnp.float32) * inverse
        up_val = jnp.dot(inner, up_mat, preferred_element_type=jnp.float32) * inverse
        return (jax.nn.silu(gate_val) * up_val).astype(jnp.bfloat16)

    term = jnp.dot(hidden(wg, wu), wd, preferred_element_type=jnp.float32)
    term = term + jnp.dot(hidden(wg2, wu2), wd2, preferred_element_type=jnp.float32)
    reduced = plane_scatter(term.astype(jnp.bfloat16), 4)
    returned = lax.all_to_all(
        reduced.reshape(experts, slots, 2 * feats), ("y", "w"), 0, 0, tiled=True
    ).reshape(experts * slots, 2 * feats)
    mixture = jnp.dot(picker_high, returned, preferred_element_type=jnp.float32)
    mixture = mixture + jnp.dot(picker_low, returned, preferred_element_type=jnp.float32)
    here = jnp.arange(2, dtype=jnp.int32)[None, :, None, None] == k
    placed = jnp.where(here, stream.reshape(2, 1, tokens, 2 * feats), 0.0)
    share = mixture + placed.reshape(block_tokens, 2 * feats)
    keep = jnp.where(k == 0, share[:, :feats], share[:, feats:])
    give = jnp.where(k == 0, share[:, feats:], share[:, :feats])
    mixed = (keep + swap(give)).astype(jnp.bfloat16)
    return (attended, mixed)


def solution(mesh):
    fine = Mesh(mesh.devices.reshape(NX, NZ, 2, 4, 2), ("x", "z", "k", "y", "w"))
    ctx, exp = ("x", "z", "k"), ("y", "w")
    in_specs = (
        P(ctx, exp),
        P(ctx, exp),
        P(ctx, exp),
        P(ctx),
        P(ctx),
        P(exp, ctx),
        P(exp, ctx),
        P(ctx),
        P(exp, None),
        P(exp, None),
        P(exp, None, ctx),
        P(exp, None, ctx),
        P(exp, ctx, None),
    )
    out_specs = (P(ctx, exp), P(exp, ctx))
    return jax.shard_map(local, mesh=fine, in_specs=in_specs, out_specs=out_specs, check_vma=False)
```

```python
import functools

import jax
import jax.numpy as jnp
from jax import lax
from jax.experimental import pallas as pl
from jax.experimental.pallas import tpu as pltpu
from jax.sharding import Mesh
from jax.sharding import PartitionSpec as P

MESH = pl.DeviceIdType.MESH
DMA = pltpu.SemaphoreType.DMA
D = 6144
NX, NZ = 4, 4
STEPS = 4
neg_big = -1e30
epsilon = 1e-05


def remote(src, dst, send_sem, recv_sem, device):
    return pltpu.make_async_remote_copy(
        src_ref=src,
        dst_ref=dst,
        send_sem=send_sem,
        recv_sem=recv_sem,
        device_id=device,
        device_id_type=MESH,
    )


def enter(devices):
    barrier = pltpu.get_barrier_semaphore()
    for device in devices:
        pl.semaphore_signal(barrier, inc=1, device_id=device, device_id_type=MESH)
    pl.semaphore_wait(barrier, len(devices))


def plane_peers(x, z):
    peers = [{"x": lax.rem(x + 1, NX)}, {"x": lax.rem(x + 3, NX)}]
    return peers + [{"z": lax.rem(z + step, NZ)} for step in range(1, NZ)]


def gather_kernel(share, cut, in_ref, out_ref, own_sem, zs, zr, xs, xr, fs, fr, ks, kr, hs, hr):
    x, z, k = lax.axis_index("x"), lax.axis_index("z"), lax.axis_index("k")
    up, down, across = lax.rem(x + 1, NX), lax.rem(x + 3, NX), lax.rem(x + 2, NX)
    rows = in_ref.shape[0]
    halves = ((0, cut), (cut, rows - cut))
    width = 2 if share else 1

    def spot(bx, bz, core, half=None):
        where = (bx * NZ + bz) * width + (core if share else 0)
        if half is None:
            return out_ref.at[where]
        return out_ref.at[where, pl.ds(*halves[half])]

    enter(plane_peers(x, z) + ([{"k": 1 - k}] if share else []))
    sent = []

    def send(src, dst, send_sem, recv_sem, device):
        copy = remote(src, dst, send_sem, recv_sem, device)
        copy.start()
        sent.append(copy)

    def arrived(ref, send_sem, recv_sem):
        remote(ref, ref, send_sem, recv_sem, {"x": up}).wait_recv()

    own = pltpu.make_async_copy(in_ref, spot(x, z, k), own_sem)
    own.start()
    for step in range(1, NZ):
        send(in_ref, spot(x, z, k), zs.at[step - 1], zr.at[step - 1], {"z": lax.rem(z + step, NZ)})
    for step in range(NZ):
        bz = lax.rem(z + NZ - step, NZ)
        dst = spot(x, bz, k)
        src = in_ref if step == 0 else dst
        if step:
            arrived(dst, zs.at[step - 1], zr.at[step - 1])
        send(src, dst, xs.at[0, step], xr.at[0, step], {"x": up})
        send(src, dst, xs.at[1, step], xr.at[1, step], {"x": down})
        if share:
            send(src, dst, ks.at[0, step], kr.at[0, step], {"k": 1 - k})
    for step in range(NZ):
        bz = lax.rem(z + NZ - step, NZ)
        for way, (came, goes) in enumerate(((down, up), (up, down))):
            block = spot(came, bz, k)
            arrived(block, xs.at[way, step], xr.at[way, step])
            half = spot(came, bz, k, way)
            send(half, half, fs.at[way, step], fr.at[way, step], {"x": goes})
            if share:
                send(block, block, ks.at[1 + way, step], kr.at[1 + way, step], {"k": 1 - k})
    for step in range(NZ):
        bz = lax.rem(z + NZ - step, NZ)
        for way in range(2):
            half = spot(across, bz, k, way)
            arrived(half, fs.at[way, step], fr.at[way, step])
            if share:
                send(half, half, hs.at[way, step], hr.at[way, step], {"k": 1 - k})
    if share:
        for step in range(NZ):
            bz = lax.rem(z + NZ - step, NZ)
            for which, bx in enumerate((x, down, up)):
                arrived(spot(bx, bz, 1 - k), ks.at[which, step], kr.at[which, step])
            for way in range(2):
                arrived(spot(across, bz, 1 - k, way), hs.at[way, step], hr.at[way, step])
    for copy in sent:
        copy.wait_send()
    own.wait()


def plane_gather(block, collective_id, share=False, cut=None):
    rows = block.shape[0]
    count = NX * NZ * (2 if share else 1)
    return pl.pallas_call(
        functools.partial(gather_kernel, share, rows // 2 if cut is None else cut),
        out_shape=jax.ShapeDtypeStruct((count,) + block.shape, block.dtype),
        in_specs=[pl.BlockSpec(memory_space=pl.ANY)],
        out_specs=pl.BlockSpec(memory_space=pl.ANY),
        scratch_shapes=[
            DMA,
            DMA((3,)),
            DMA((3,)),
            DMA((2, 4)),
            DMA((2, 4)),
            DMA((2, 4)),
            DMA((2, 4)),
            DMA((3, 4)),
            DMA((3, 4)),
            DMA((2, 4)),
            DMA((2, 4)),
        ],
        compiler_params=pltpu.CompilerParams(
            collective_id=collective_id, has_side_effects=True, vmem_limit_bytes=16 << 20
        ),
        name=f"plane_gather_{collective_id}",
    )(block)


def expert_kernel(
    row_ref, gain_ref, wg_ref, wg2_ref, wu_ref, wu2_ref, wd_ref, wd2_ref, out_ref,
    rows_in, spread, part, relay, from_x, mine, from_z, done, wg, wu, wd, gate_sum, up_sum, squares, act,
    w_sem, own_sem, back_sem, ds, dr, zs, zr, xs, xr, fs, fr, rs, rr, us, ur, vs, vr, qs, qr, os, orr,
):
    x, z, y, w = (lax.axis_index(name) for name in ("x", "z", "y", "w"))
    up, down, across = lax.rem(x + 1, NX), lax.rem(x + 3, NX), lax.rem(x + 2, NX)
    slots, width = row_ref.shape[1], row_ref.shape[2]
    rows = 2 * slots
    half = rows // 2
    own_block = pl.ds(pl.multiple_of((x * NZ + z) * width, 128), width)
    ways = (up, down)
    order = [lax.rem(z + step, NZ) for step in (1, 2, 3, 0)]
    others = [(dy, dw) for dy in range(STEPS) for dw in range(2) if (dy, dw) != (0, 0)]

    def remote_start(src, dst, send_sem, recv_sem, device):
        remote(src, dst, send_sem, recv_sem, device).start()

    def arrived(ref, send_sem, recv_sem):
        remote(ref, ref, send_sem, recv_sem, {"x": up}).wait_recv()

    def left(ref, send_sem, recv_sem):
        remote(ref, ref, send_sem, recv_sem, {"x": up}).wait_send()

    def source(t):
        return lax.rem(y + t, STEPS)

    def cols(bx, bz):
        return pl.ds(pl.multiple_of((bx * NZ + bz) * width, 128), width)

    loads = [
        pltpu.make_async_copy(src, dst, w_sem.at[i])
        for i, (src, dst) in enumerate(
            (
                (wg_ref, wg.at[:, pl.ds(0, 256)]),
                (wg2_ref, wg.at[:, pl.ds(256, 256)]),
                (wu_ref, wu.at[:, pl.ds(0, 256)]),
                (wu2_ref, wu.at[:, pl.ds(256, 256)]),
                (wd_ref, wd.at[pl.ds(0, 256)]),
                (wd2_ref, wd.at[pl.ds(256, 256)]),
            )
        )
    ]
    peers = plane_peers(x, z)
    peers += [{"y": lax.rem(y + dy, STEPS), "w": lax.rem(w + dw, 2)} for dy, dw in others]
    enter(peers)

    for dy, dw in others:
        ty, tw = lax.rem(y + dy, STEPS), lax.rem(w + dw, 2)
        remote_start(
            row_ref.at[2 * ty + tw],
            rows_in.at[y, pl.ds(w * slots, slots)],
            ds.at[2 * dy + dw],
            dr.at[2 * dy + dw],
            {"y": ty, "w": tw},
        )
    own_rows = pltpu.make_async_copy(
        row_ref.at[2 * y + w], rows_in.at[y, pl.ds(w * slots, slots)], own_sem.at[STEPS]
    )
    own_rows.start()
    for load in loads:
        load.start()

    def keep_own(t):
        ys = source(t)
        return pltpu.make_async_copy(rows_in.at[ys], spread.at[ys, :, own_block], own_sem.at[t])

    def begin(t):
        ys = source(t)
        dy = lax.rem(STEPS - t, STEPS)
        for dw in range(2):
            piece = rows_in.at[ys, pl.ds(lax.rem(w + dw, 2) * slots, slots)]
            if dw == 0:

                @pl.when(t == 0)
                def _():
                    own_rows.wait()

                @pl.when(t > 0)
                def _():
                    arrived(piece, ds.at[2 * dy], dr.at[2 * dy])

            else:
                arrived(piece, ds.at[2 * dy + dw], dr.at[2 * dy + dw])
        keep_own(t).start()
        src, dst = rows_in.at[ys], spread.at[ys, :, own_block]
        for step in range(1, NZ):
            at = t * 3 + step - 1
            remote_start(src, dst, zs.at[at], zr.at[at], {"z": lax.rem(z + step, NZ)})
        for way, goes in enumerate(ways):
            at = t * 8 + way * 4
            remote_start(src, dst, xs.at[at], xr.at[at], {"x": goes})

    def along_x(t):
        ys = source(t)
        for step in range(1, NZ):
            block = spread.at[ys, :, cols(x, lax.rem(z + NZ - step, NZ))]
            arrived(block, zs.at[t * 3 + step - 1], zr.at[t * 3 + step - 1])
            for way, goes in enumerate(ways):
                at = t * 8 + way * 4 + step
                remote_start(block, block, xs.at[at], xr.at[at], {"x": goes})

    def pass_on(t):
        ys = source(t)
        for step in range(NZ):
            bz = lax.rem(z + NZ - step, NZ)
            for way, (came, goes) in enumerate(((down, up), (up, down))):
                at = t * 8 + way * 4 + step
                arrived(spread.at[ys, :, cols(came, bz)], xs.at[at], xr.at[at])
                piece = spread.at[ys, pl.ds(way * half, half), cols(came, bz)]
                remote_start(piece, piece, fs.at[at], fr.at[at], {"x": goes})

    def complete(t):
        ys = source(t)
        for step in range(NZ):
            bz = lax.rem(z + NZ - step, NZ)
            for way in range(2):
                at = t * 8 + way * 4 + step
                arrived(spread.at[ys, pl.ds(way * half, half), cols(across, bz)], fs.at[at], fr.at[at])
        keep_own(t).wait()

    deep = 768

    def hidden(t):
        ys = source(t)
        gate_sum[...] = jnp.zeros_like(gate_sum)
        up_sum[...] = jnp.zeros_like(up_sum)
        squares[...] = jnp.zeros_like(squares)

        @pl.loop(0, D // deep)
        def _(i):
            at = pl.ds(pl.multiple_of(i * deep, 128), deep)
            piece = spread[ys, :, at]
            gate_sum[...] += jnp.dot(piece, wg[at, :], preferred_element_type=jnp.float32)
            up_sum[...] += jnp.dot(piece, wu[at, :], preferred_element_type=jnp.float32)
            wide = piece.astype(jnp.float32)
            wide = wide * wide * gain_ref[:, at]
            total = wide[:, :128]
            for lane in range(128, deep, 128):
                total = total + wide[:, lane : lane + 128]
            squares[...] += total

        tile = 48

        @pl.loop(0, rows // tile)
        def _(i):
            at = pl.ds(i * tile, tile)
            inverse = lax.rsqrt(jnp.sum(squares[at, :], axis=1, keepdims=True) / D + epsilon)
            gate = gate_sum[at, :] * inverse
            act[at, :] = (gate / (1.0 + jnp.exp(-gate)) * (up_sum[at, :] * inverse)).astype(act.dtype)

    def project(t, bx):
        ys = source(t)
        for i in range(NZ * width // deep):
            at = pl.ds(pl.multiple_of(bx * (NZ * width) + i * deep, 128), deep)
            part[ys, :, at] = jnp.dot(
                act[...], wd[:, at], preferred_element_type=jnp.float32
            ).astype(part.dtype)

    def give(t):
        ys = source(t)
        project(t, across)
        for step in range(NZ):
            for way, goes in enumerate(ways):
                at = t * 8 + way * 4 + step
                remote_start(
                    part.at[ys, pl.ds(way * half, half), cols(across, order[step])],
                    relay.at[ys, way, step],
                    rs.at[at],
                    rr.at[at],
                    {"x": goes},
                )
        for way, goes in enumerate(ways):
            project(t, goes)
            for step in range(NZ):
                at = t * 8 + way * 4 + step
                remote_start(
                    part.at[ys, pl.ds((1 - way) * half, half), cols(goes, order[step])],
                    from_x.at[ys, way, step, pl.ds((1 - way) * half, half)],
                    us.at[at],
                    ur.at[at],
                    {"x": goes},
                )
        project(t, x)

    tile = 48

    def add(dst, terms, count):
        @pl.loop(0, count // tile)
        def _(i):
            at = pl.ds(i * tile, tile)
            total = terms[0][at, :].astype(jnp.float32)
            for term in terms[1:]:
                total = total + term[at, :].astype(jnp.float32)
            dst[at, :] = total.astype(dst.dtype)

    def add_relayed(t):
        ys = source(t)
        for step in range(NZ):
            for way, goes in enumerate(ways):
                at = t * 8 + way * 4 + step
                held = relay.at[ys, way, step]
                arrived(held, rs.at[at], rr.at[at])
                add(held, (held, part.at[ys, pl.ds(way * half, half), cols(goes, order[step])]), half)
                remote_start(
                    held,
                    from_x.at[ys, way, step, pl.ds(way * half, half)],
                    vs.at[at],
                    vr.at[at],
                    {"x": goes},
                )

    def add_x(t):
        ys = source(t)
        for step in range(NZ):
            for way in range(2):
                at = t * 8 + way * 4 + step
                held = from_x.at[ys, way, step]
                arrived(held.at[pl.ds(way * half, half)], vs.at[at], vr.at[at])
                arrived(held.at[pl.ds((1 - way) * half, half)], us.at[at], ur.at[at])
            own = part.at[ys, :, cols(x, order[step])]
            add(mine.at[ys, step], (own, from_x.at[ys, 0, step], from_x.at[ys, 1, step]), rows)
            if step < NZ - 1:
                at = t * 3 + step
                remote_start(mine.at[ys, step], from_z.at[ys, step], qs.at[at], qr.at[at], {"z": order[step]})

    def back(t):
        ys = source(t)
        return pltpu.make_async_copy(done.at[ys, pl.ds(w * slots, slots)], out_ref.at[2 * y + w], back_sem)

    def add_z(t):
        ys = source(t)
        for step in range(NZ - 1):
            at = t * 3 + step
            arrived(from_z.at[ys, step], qs.at[at], qr.at[at])
        add(done.at[ys], [mine.at[ys, NZ - 1]] + [from_z.at[ys, i] for i in range(NZ - 1)], rows)
        for dw in range(2):
            tw = lax.rem(w + dw, 2)
            piece = done.at[ys, pl.ds(tw * slots, slots)]

            def go():
                remote_start(
                    piece, out_ref.at[2 * y + w], os.at[2 * t + dw], orr.at[2 * t + dw], {"y": ys, "w": tw}
                )

            if dw == 0:
                pl.when(t > 0)(go)

                @pl.when(t == 0)
                def _():
                    back(t).start()

            else:
                go()

    begin(0)
    begin(1)

    @pl.loop(0, STEPS + 5)
    def _(t):
        def stage(offset, what):
            @pl.when((t >= offset) & (t - offset < STEPS))
            def _():
                what(t - offset)

        stage(0, along_x)

        @pl.when(t + 2 < STEPS)
        def _():
            begin(t + 2)

        stage(1, pass_on)
        stage(4, add_x)
        stage(5, add_z)

        @pl.when(t == 2)
        def _():
            for load in loads:
                load.wait()

        def first(c):
            complete(c)
            hidden(c)

        stage(2, first)
        stage(3, add_relayed)
        stage(2, give)

    back(0).wait()
    for dy, dw in others:
        j = 2 * dy + dw
        fy, fw = lax.rem(y + STEPS - dy, STEPS), lax.rem(w + dw, 2)
        arrived(out_ref.at[2 * fy + fw], os.at[j], orr.at[j])
    for dy, dw in others:
        j = 2 * dy + dw
        left(row_ref.at[0], ds.at[j], dr.at[j])
        left(row_ref.at[0], os.at[j], orr.at[j])

    @pl.loop(0, STEPS)
    def _(t):
        for i in range(NZ - 1):
            at = t * 3 + i
            left(rows_in.at[0], zs.at[at], zr.at[at])
            left(rows_in.at[0], qs.at[at], qr.at[at])
        for i in range(8):
            at = t * 8 + i
            left(rows_in.at[0], xs.at[at], xr.at[at])
            for s, r in ((fs, fr), (rs, rr), (us, ur), (vs, vr)):
                left(rows_in.at[0, pl.ds(0, half)], s.at[at], r.at[at])


def expert_call(outgoing, gain_squares, weights, collective_id):
    experts, slots, width = outgoing.shape
    rows, kind = 2 * slots, outgoing.dtype
    hidden = 2 * weights[0].shape[1]
    any_spec, vmem_spec = pl.BlockSpec(memory_space=pl.ANY), pl.BlockSpec(memory_space=pltpu.VMEM)
    flops = 2 * STEPS * rows * D * hidden * 3
    return pl.pallas_call(
        expert_kernel,
        out_shape=jax.ShapeDtypeStruct(outgoing.shape, kind),
        in_specs=[any_spec, vmem_spec] + [any_spec] * 6,
        out_specs=vmem_spec,
        scratch_shapes=[
            pltpu.VMEM((STEPS, rows, width), kind),
            pltpu.VMEM((STEPS, rows, D), kind),
            pltpu.VMEM((STEPS, rows, D), kind),
            pltpu.VMEM((STEPS, 2, NZ, rows // 2, width), kind),
            pltpu.VMEM((STEPS, 2, NZ, rows, width), kind),
            pltpu.VMEM((STEPS, NZ, rows, width), kind),
            pltpu.VMEM((STEPS, NZ - 1, rows, width), kind),
            pltpu.VMEM((STEPS, rows, width), kind),
            pltpu.VMEM((D, hidden), kind),
            pltpu.VMEM((D, hidden), kind),
            pltpu.VMEM((hidden, D), kind),
            pltpu.VMEM((rows, hidden), jnp.float32),
            pltpu.VMEM((rows, hidden), jnp.float32),
            pltpu.VMEM((rows, 128), jnp.float32),
            pltpu.VMEM((rows, hidden), kind),
            DMA((6,)),
            DMA((STEPS + 1,)),
            DMA,
        ]
        + [DMA((8,))] * 2
        + [DMA((3 * STEPS,))] * 2
        + [DMA((8 * STEPS,))] * 10
        + [DMA((3 * STEPS,))] * 2
        + [DMA((8,))] * 2,
        compiler_params=pltpu.CompilerParams(
            collective_id=collective_id, has_side_effects=True, vmem_limit_bytes=60 << 20
        ),
        cost_estimate=pl.CostEstimate(flops=flops, bytes_accessed=20 << 20, transcendentals=0),
        name=f"expert_{collective_id}",
    )(outgoing, gain_squares, *weights)


def swap(array):
    return lax.ppermute(array, "k", [(0, 1), (1, 0)])


def beside(own, other, k, axis):
    return jnp.where(
        k == 0,
        jnp.concatenate([own, other], axis=axis),
        jnp.concatenate([other, own], axis=axis),
    )


def local(
    queries,
    rotated_key_cache,
    value_cache_rows,
    kv_pos,
    q_pos,
    residual,
    w_out,
    norm_gain,
    routes,
    gate_probs,
    w_gate,
    w_up,
    w_down,
):
    k = lax.axis_index("k")
    chip = lax.axis_index("x") * NZ + lax.axis_index("z")
    tokens, head_dim = queries.shape[0], rotated_key_cache.shape[1]
    heads = queries.shape[1] // head_dim
    feats = residual.shape[1]
    block_tokens = residual.shape[0]

    wg, wu, wd = w_gate[0], w_up[0], w_down[0]
    wg2, wu2, wd2 = swap(wg), swap(wu), swap(wd)
    w_out2 = beside(w_out, swap(w_out), k, 1)
    by_core = residual.reshape(2, 2, tokens, feats)
    res_own = lax.dynamic_index_in_dim(by_core, k, 1, keepdims=False).reshape(2 * tokens, feats)
    res_give = lax.dynamic_index_in_dim(by_core, 1 - k, 1, keepdims=False).reshape(2 * tokens, feats)
    res = beside(res_own, swap(res_give), k, 1)

    pages = (kv_pos.reshape(2, 128)[:, 0] // 128).astype(jnp.bfloat16)
    extra = jnp.zeros((16, 2 * head_dim), jnp.bfloat16)
    extra = extra.at[0, :2].set(pages).at[1, :feats].set(norm_gain)
    block = jnp.concatenate(
        [jnp.concatenate([rotated_key_cache, value_cache_rows], axis=1), extra], axis=0
    )
    gathered = plane_gather(block, 1, share=True, cut=144)
    keys = gathered[:, :256, :head_dim].reshape(-1, head_dim)
    values = gathered[:, :256, head_dim:].reshape(-1, head_dim)
    starts = gathered[:, 256, :2].astype(jnp.int32) * 128
    positions = (starts.reshape(-1, 1) + jnp.arange(128, dtype=jnp.int32)[None, :]).reshape(-1)
    gains = gathered[:, 257, :feats].astype(jnp.float32).reshape(-1)

    rows = queries.reshape(tokens * heads, head_dim)
    row_pos = jnp.repeat(q_pos, heads)
    scores = lax.dot_general(
        rows, keys, (((1,), (1,)), ((), ())), preferred_element_type=jnp.float32
    ) * (head_dim**-0.5)
    scores = jnp.where(positions[None, :] <= row_pos[:, None], scores, neg_big)
    weights = jnp.exp(scores - jnp.max(scores, axis=1, keepdims=True))
    totals = jnp.sum(weights, axis=1, keepdims=True)
    blended = jnp.dot(weights.astype(jnp.bfloat16), values, preferred_element_type=jnp.float32)
    attended = (blended / totals).reshape(tokens, heads * head_dim).astype(jnp.bfloat16)

    slab = plane_gather(attended, 2).reshape(NX * NZ * tokens, heads * head_dim)
    projected = jnp.dot(slab, w_out2, preferred_element_type=jnp.float32).astype(jnp.bfloat16)
    pieces = lax.all_to_all(
        projected.reshape(8, 2 * tokens, 2 * feats), ("y", "w"), 0, 0, tiled=True
    )
    stream = res.astype(jnp.float32) + jnp.sum(pieces.astype(jnp.float32), axis=0)

    own_gain = lax.dynamic_slice_in_dim(gains, chip * 2 * feats, 2 * feats)
    scaled = (stream * own_gain[None, :]).astype(jnp.bfloat16)
    both = beside(
        scaled.reshape(2, 1, tokens, 2 * feats), swap(scaled).reshape(2, 1, tokens, 2 * feats), k, 1
    ).reshape(block_tokens, 2 * feats)

    experts, choices = 8, routes.shape[1]
    slots = 6 * block_tokens // experts // 2
    flat_ids = routes.reshape(-1)
    onehot = (flat_ids[:, None] == jnp.arange(experts, dtype=jnp.int32)[None, :]).astype(jnp.int32)
    earlier = jnp.cumsum(onehot, axis=0) - onehot
    slot = jnp.sum(earlier * onehot, axis=1) - k * slots
    cell = jnp.where((slot >= 0) & (slot < slots), flat_ids * slots + slot, -1)
    layout = cell[:, None] == jnp.arange(experts * slots, dtype=jnp.int32)[None, :]
    layout = layout.reshape(block_tokens, choices, experts * slots)
    placer = jnp.any(layout, axis=1).astype(jnp.bfloat16)
    picker = jnp.sum(jnp.where(layout, gate_probs[:, :, None], 0.0), axis=1)
    picker_high = picker.astype(jnp.bfloat16)
    picker_low = (picker - picker_high.astype(jnp.float32)).astype(jnp.bfloat16)

    outgoing = lax.dot_general(
        placer, both, (((0,), (0,)), ((), ())), preferred_element_type=jnp.float32
    ).astype(jnp.bfloat16)
    returned = expert_call(
        outgoing.reshape(experts, slots, 2 * feats),
        (1.0 / (gains * gains))[None, :],
        (wg, wg2, wu, wu2, wd, wd2),
        3,
    ).reshape(experts * slots, 2 * feats)
    mixture = jnp.dot(picker_high, returned, preferred_element_type=jnp.float32)
    mixture = mixture + jnp.dot(picker_low, returned, preferred_element_type=jnp.float32)
    here = jnp.arange(2, dtype=jnp.int32)[None, :, None, None] == k
    placed = jnp.where(here, stream.reshape(2, 1, tokens, 2 * feats), 0.0)
    share = mixture + placed.reshape(block_tokens, 2 * feats)
    keep = jnp.where(k == 0, share[:, :feats], share[:, feats:])
    give = jnp.where(k == 0, share[:, feats:], share[:, :feats])
    mixed = (keep + swap(give)).astype(jnp.bfloat16)
    return (attended, mixed)


def solution(mesh):
    fine = Mesh(mesh.devices.reshape(NX, NZ, 2, 4, 2), ("x", "z", "k", "y", "w"))
    ctx, exp = ("x", "z", "k"), ("y", "w")
    in_specs = (
        P(ctx, exp),
        P(ctx, exp),
        P(ctx, exp),
        P(ctx),
        P(ctx),
        P(exp, ctx),
        P(exp, ctx),
        P(ctx),
        P(exp, None),
        P(exp, None),
        P(exp, None, ctx),
        P(exp, None, ctx),
        P(exp, ctx, None),
    )
    out_specs = (P(ctx, exp), P(exp, ctx))
    return jax.shard_map(local, mesh=fine, in_specs=in_specs, out_specs=out_specs, check_vma=False)
```

```python
import functools

import jax
import jax.numpy as jnp
from jax import lax
from jax.experimental import pallas as pl
from jax.experimental.pallas import tpu as pltpu
from jax.sharding import Mesh
from jax.sharding import PartitionSpec as P

MESH = pl.DeviceIdType.MESH
DMA = pltpu.SemaphoreType.DMA
D = 6144
NX, NZ = 4, 4
STEPS = 8
neg_big = -1e30
epsilon = 1e-05


def remote(src, dst, send_sem, recv_sem, device):
    return pltpu.make_async_remote_copy(
        src_ref=src,
        dst_ref=dst,
        send_sem=send_sem,
        recv_sem=recv_sem,
        device_id=device,
        device_id_type=MESH,
    )


def enter(devices):
    barrier = pltpu.get_barrier_semaphore()
    for device in devices:
        pl.semaphore_signal(barrier, inc=1, device_id=device, device_id_type=MESH)
    pl.semaphore_wait(barrier, len(devices))


def plane_peers(x, z):
    peers = [{"x": lax.rem(x + 1, NX)}, {"x": lax.rem(x + 3, NX)}]
    return peers + [{"z": lax.rem(z + step, NZ)} for step in range(1, NZ)]


def attend_kernel(
    q_ref, pos_ref, k_ref, v_ref, page_ref, gain_ref, out_ref, extra_ref,
    held, q_rows, top, acc, zs, zr, xs, xr, fs, fr, ks, kr, hs, hr,
):
    x, z, k = (lax.axis_index(name) for name in ("x", "z", "k"))
    up, down, across = lax.rem(x + 1, NX), lax.rem(x + 3, NX), lax.rem(x + 2, NX)
    ways = (up, down)
    tokens, head = out_ref.shape[0], k_ref.shape[1]
    heads = out_ref.shape[1] // head
    count = k_ref.shape[0]
    rows = tokens * heads
    halves = ((0, 144), (144, held.shape[1] - 144))

    own = 2 * (x * NZ + z) + k
    held[own, :count, :head] = k_ref[...]
    held[own, :count, head:] = v_ref[...]
    pages = page_ref[...].astype(jnp.float32) * (1.0 / 128.0)
    row = lax.broadcasted_iota(jnp.int32, (16, 2 * head), 0)
    lane = lax.broadcasted_iota(jnp.int32, (16, 2 * head), 1)
    numbers = jnp.where(lane == 0, pages[0:1, 0:1], jnp.where(lane == 1, pages[1:2, 0:1], 0.0))
    extra = jnp.where(row == 0, numbers, jnp.where(row == 1, gain_ref[...], 0.0))
    held[own, count:, :] = extra.astype(held.dtype)
    enter(plane_peers(x, z) + [{"k": 1 - k}])

    def spot(bx, bz, core, half=None):
        where = 2 * (bx * NZ + bz) + core
        if half is None:
            return held.at[where]
        return held.at[where, pl.ds(*halves[half])]

    def send(ref, send_sem, recv_sem, device):
        remote(ref, ref, send_sem, recv_sem, device).start()

    def arrived(ref, send_sem, recv_sem):
        remote(ref, ref, send_sem, recv_sem, {"x": up}).wait_recv()

    def left(ref, send_sem, recv_sem):
        remote(ref, ref, send_sem, recv_sem, {"x": up}).wait_send()

    mine = spot(x, z, k)
    for step in range(1, NZ):
        send(mine, zs.at[step - 1], zr.at[step - 1], {"z": lax.rem(z + step, NZ)})
    for way, goes in enumerate(ways):
        send(mine, xs.at[4 * way], xr.at[4 * way], {"x": goes})
    send(mine, ks.at[0], kr.at[0], {"k": 1 - k})

    for h in range(heads):
        q_rows[pl.ds(h * tokens, tokens), :] = q_ref[:, pl.ds(h * head, head)]
    top[...] = jnp.full_like(top, neg_big)
    acc[...] = jnp.zeros_like(acc)
    scaling = head**-0.5 * 1.4426950408889634
    tile = 128

    def attend(bx, bz):
        where = 2 * (bx * NZ + bz)
        terms = []
        steps = lax.broadcasted_iota(jnp.int32, (1, head), 1).astype(jnp.float32)
        for core in range(2):
            numbers = held[where + core, count:, :head].astype(jnp.float32)
            positions = jnp.concatenate(
                [numbers[0:1, 0:1] * 128.0 + steps, numbers[0:1, 1:2] * 128.0 + steps], axis=1
            )
            terms.append((held[where + core, :count, :head], held[where + core, :count, head:], positions))
        ones = jnp.ones((count, head), held.dtype)
        for r in range(rows // tile):
            at = pl.ds(r * tile, tile)
            scores = []
            for keys, _, positions in terms:
                score = lax.dot_general(
                    q_rows[at, :], keys, (((1,), (1,)), ((), ())), preferred_element_type=jnp.float32
                )
                scores.append(jnp.where(positions <= pos_ref[at, :], score * scaling, neg_big))
            high = jnp.maximum(scores[0], scores[1])
            high = jnp.max(jnp.maximum(high[:, :head], high[:, head:]), axis=1, keepdims=True)
            old = top[at, :]
            new = jnp.maximum(old, high)
            top[at, :] = new
            fade = jnp.exp2(old - new)
            total = acc[at, :] * jnp.concatenate([fade, fade], axis=1)
            new = jnp.concatenate([new, new], axis=1)
            for score, (_, values, _) in zip(scores, terms):
                weights = jnp.exp2(score - new).astype(held.dtype)
                total = total + jnp.dot(
                    weights, jnp.concatenate([values, ones], axis=1), preferred_element_type=jnp.float32
                )
            acc[at, :] = total

    arrived(spot(x, z, 1 - k), ks.at[0], kr.at[0])
    attend(x, z)

    @pl.loop(1, NZ)
    def _(step):
        ref = spot(x, lax.rem(z + NZ - step, NZ), k)
        arrived(ref, zs.at[step - 1], zr.at[step - 1])
        for way, goes in enumerate(ways):
            send(ref, xs.at[4 * way + step], xr.at[4 * way + step], {"x": goes})
        send(ref, ks.at[step], kr.at[step], {"k": 1 - k})

    @pl.loop(0, NZ)
    def _(step):
        bz = lax.rem(z + NZ - step, NZ)
        for way, (came, goes) in enumerate(((down, up), (up, down))):
            at = 4 * way + step
            ref = spot(came, bz, k)
            arrived(ref, xs.at[at], xr.at[at])
            send(spot(came, bz, k, way), fs.at[at], fr.at[at], {"x": goes})
            send(ref, ks.at[4 + at], kr.at[4 + at], {"k": 1 - k})

        @pl.when(step > 0)
        def _():
            arrived(spot(x, bz, 1 - k), ks.at[step], kr.at[step])
            attend(x, bz)

    @pl.loop(0, NZ)
    def _(step):
        bz = lax.rem(z + NZ - step, NZ)
        for way in range(2):
            at = 4 * way + step
            ref = spot(across, bz, k, way)
            arrived(ref, fs.at[at], fr.at[at])
            send(ref, hs.at[at], hr.at[at], {"k": 1 - k})
        for way, came in enumerate((down, up)):
            at = 4 + 4 * way + step
            arrived(spot(came, bz, 1 - k), ks.at[at], kr.at[at])
            attend(came, bz)

    @pl.loop(0, NZ)
    def _(step):
        bz = lax.rem(z + NZ - step, NZ)
        for way in range(2):
            at = 4 * way + step
            arrived(spot(across, bz, 1 - k, way), hs.at[at], hr.at[at])
        attend(across, bz)

    for h in range(heads):
        at = pl.ds(h * tokens, tokens)
        out_ref[:, pl.ds(h * head, head)] = (acc[at, :head] / acc[at, head:]).astype(out_ref.dtype)
    extra_ref[...] = held[:, count:, :]
    for i in range(NZ - 1):
        left(mine, zs.at[i], zr.at[i])

    @pl.loop(0, NZ)
    def _(step):
        left(mine, ks.at[step], kr.at[step])
        for way in range(2):
            at = 4 * way + step
            left(mine, xs.at[at], xr.at[at])
            left(mine, ks.at[4 + at], kr.at[4 + at])
            left(spot(x, z, k, way), fs.at[at], fr.at[at])
            left(spot(x, z, k, way), hs.at[at], hr.at[at])


def attend_call(queries, row_pos, keys, values, kv_pos, gain, collective_id):
    kind = queries.dtype
    tokens, head = queries.shape[0], keys.shape[1]
    rows = queries.shape[1] // head * tokens
    vmem_spec = pl.BlockSpec(memory_space=pltpu.VMEM)
    blocks = 2 * NX * NZ
    deep = keys.shape[0] + 16
    return pl.pallas_call(
        attend_kernel,
        out_shape=(
            jax.ShapeDtypeStruct(queries.shape, kind),
            jax.ShapeDtypeStruct((blocks, 16, 2 * head), kind),
        ),
        in_specs=[vmem_spec] * 6,
        out_specs=(vmem_spec, vmem_spec),
        scratch_shapes=[
            pltpu.VMEM((blocks, deep, 2 * head), kind),
            pltpu.VMEM((rows, head), kind),
            pltpu.VMEM((rows, head), jnp.float32),
            pltpu.VMEM((rows, 2 * head), jnp.float32),
            DMA((3,)),
            DMA((3,)),
        ]
        + [DMA((8,))] * 4
        + [DMA((12,))] * 2
        + [DMA((8,))] * 2,
        compiler_params=pltpu.CompilerParams(
            collective_id=collective_id, has_side_effects=True, vmem_limit_bytes=24 << 20
        ),
        name=f"attend_{collective_id}",
    )(queries, row_pos, keys, values, kv_pos, gain)


def expert_kernel(
    att_ref, wo_ref, res_ref, scale_ref, placer_ref,
    gain_ref, wg_ref, wg2_ref, wu_ref, wu2_ref, wd_ref, wd2_ref, out_ref, stream_ref,
    slab, leaving, pieces, both, row_ref, azs, azr, axs, axr, afs, afr, ps, pr, bs, br,
    rows_in, spread, part, relay, from_x, mine, from_z, done, wg, wu, wd, gate_sum, up_sum, squares, act,
    w_sem, own_sem, back_sem, ds, dr, zs, zr, xs, xr, fs, fr, rs, rr, us, ur, vs, vr, qs, qr, os, orr,
):
    x, z, k, y, w = (lax.axis_index(name) for name in ("x", "z", "k", "y", "w"))
    up, down, across = lax.rem(x + 1, NX), lax.rem(x + 3, NX), lax.rem(x + 2, NX)
    slots, width = row_ref.shape[1], row_ref.shape[2]
    rows = slots
    half = rows // 2
    own_block = pl.ds(pl.multiple_of((x * NZ + z) * width, 128), width)
    ways = (up, down)
    order = [lax.rem(z + step, NZ) for step in (1, 2, 3, 0)]
    others = [(dy, dw) for dy in range(4) for dw in range(2) if (dy, dw) != (0, 0)]

    def remote_start(src, dst, send_sem, recv_sem, device):
        remote(src, dst, send_sem, recv_sem, device).start()

    def arrived(ref, send_sem, recv_sem):
        remote(ref, ref, send_sem, recv_sem, {"x": up}).wait_recv()

    def left(ref, send_sem, recv_sem):
        remote(ref, ref, send_sem, recv_sem, {"x": up}).wait_send()

    def place(t):
        return lax.rem(y + t // 2, 4), lax.rem(w + t, 2)

    def source(t):
        sy, sw = place(t)
        return 2 * sy + sw

    def cols(bx, bz):
        return pl.ds(pl.multiple_of((bx * NZ + bz) * width, 128), width)

    loads = [
        pltpu.make_async_copy(src, dst, w_sem.at[i])
        for i, (src, dst) in enumerate(
            (
                (wg_ref, wg.at[:, pl.ds(0, 256)]),
                (wg2_ref, wg.at[:, pl.ds(256, 256)]),
                (wu_ref, wu.at[:, pl.ds(0, 256)]),
                (wu2_ref, wu.at[:, pl.ds(256, 256)]),
                (wd_ref, wd.at[pl.ds(0, 256)]),
                (wd2_ref, wd.at[pl.ds(256, 256)]),
            )
        )
    ]
    peers = plane_peers(x, z)
    peers += [{"y": lax.rem(y + dy, 4), "w": lax.rem(w + dw, 2)} for dy, dw in others]
    enter(peers + [{"k": 1 - k}])
    for load in loads:
        load.start()

    tokens = att_ref.shape[0]

    def spot(bx, bz, way=None):
        start = pl.multiple_of((bx * NZ + bz) * tokens, 16)
        if way is None:
            return slab.at[pl.ds(start, tokens)]
        return slab.at[pl.ds(pl.multiple_of(start + way * (tokens // 2), 16), tokens // 2)]

    slab[pl.ds(pl.multiple_of((x * NZ + z) * tokens, 16), tokens), :] = att_ref[...]
    block = spot(x, z)
    for step in range(1, NZ):
        remote_start(block, block, azs.at[step - 1], azr.at[step - 1], {"z": lax.rem(z + step, NZ)})
    for way, goes in enumerate(ways):
        remote_start(block, block, axs.at[4 * way], axr.at[4 * way], {"x": goes})
    for step in range(1, NZ):
        ref = spot(x, lax.rem(z + NZ - step, NZ))
        arrived(ref, azs.at[step - 1], azr.at[step - 1])
        for way, goes in enumerate(ways):
            at = 4 * way + step
            remote_start(ref, ref, axs.at[at], axr.at[at], {"x": goes})

    both_rows = 2 * tokens

    def project_rows(bx):
        at = pl.ds(pl.multiple_of(bx * (NZ * tokens), 16), NZ * tokens)
        leaving[bx] = jnp.dot(slab[at, :], wo_ref[...], preferred_element_type=jnp.float32).astype(
            leaving.dtype
        )
        for tw in range(2):
            piece = leaving.at[bx, pl.ds(tw * both_rows, both_rows)]
            here = (bx == y) & (tw == w)

            @pl.when(here)
            def _():
                pieces[2 * y + w] = leaving[bx, tw * both_rows : (tw + 1) * both_rows, :]

            @pl.when(jnp.logical_not(here))
            def _():
                remote_start(
                    piece, pieces.at[2 * y + w], ps.at[2 * bx + tw], pr.at[2 * y + w], {"y": bx, "w": tw}
                )

    project_rows(x)
    for step in range(NZ):
        bz = lax.rem(z + NZ - step, NZ)
        for way, (came, goes) in enumerate(((down, up), (up, down))):
            at = 4 * way + step
            arrived(spot(came, bz), axs.at[at], axr.at[at])
            ref = spot(came, bz, way)
            remote_start(ref, ref, afs.at[at], afr.at[at], {"x": goes})
    project_rows(up)
    project_rows(down)
    for step in range(NZ):
        bz = lax.rem(z + NZ - step, NZ)
        for way in range(2):
            at = 4 * way + step
            arrived(spot(across, bz, way), afs.at[at], afr.at[at])
    project_rows(across)

    for dy, dw in others:
        source_of = 2 * lax.rem(y + dy, 4) + lax.rem(w + dw, 2)
        arrived(pieces.at[source_of], ps.at[source_of], pr.at[source_of])
    total = res_ref[...].astype(jnp.float32)
    for i in range(8):
        total = total + pieces[i].astype(jnp.float32)
    stream_ref[...] = total
    mine_at = pl.ds(pl.multiple_of(k * both_rows, 16), both_rows)
    both[mine_at, :] = (total * scale_ref[...]).astype(both.dtype)
    remote_start(both.at[mine_at], both.at[mine_at], bs, br, {"k": 1 - k})
    arrived(both.at[pl.ds(pl.multiple_of((1 - k) * both_rows, 16), both_rows)], bs, br)

    def place_rows(expert):
        at = pl.ds(pl.multiple_of(expert * slots, 16), slots)
        return jnp.dot(placer_ref[at, :], both[...], preferred_element_type=jnp.float32).astype(row_ref.dtype)

    rows_in[2 * y + w] = place_rows(2 * y + w)
    for dy, dw in others:
        ty, tw = lax.rem(y + dy, 4), lax.rem(w + dw, 2)
        row_ref[2 * ty + tw] = place_rows(2 * ty + tw)
        remote_start(
            row_ref.at[2 * ty + tw],
            rows_in.at[2 * y + w],
            ds.at[2 * dy + dw],
            dr.at[2 * dy + dw],
            {"y": ty, "w": tw},
        )

    def keep_own(t):
        ys = source(t)
        return pltpu.make_async_copy(rows_in.at[ys], spread.at[ys, :, own_block], own_sem.at[t])

    def begin(t):
        ys = source(t)
        j = 2 * lax.rem(4 - t // 2, 4) + lax.rem(t, 2)

        @pl.when(t > 0)
        def _():
            arrived(rows_in.at[ys], ds.at[j], dr.at[j])

        keep_own(t).start()
        src, dst = rows_in.at[ys], spread.at[ys, :, own_block]
        for step in range(1, NZ):
            at = t * 3 + step - 1
            remote_start(src, dst, zs.at[at], zr.at[at], {"z": lax.rem(z + step, NZ)})
        for way, goes in enumerate(ways):
            at = t * 8 + way * 4
            remote_start(src, dst, xs.at[at], xr.at[at], {"x": goes})

    def along_x(t):
        ys = source(t)
        for step in range(1, NZ):
            block = spread.at[ys, :, cols(x, lax.rem(z + NZ - step, NZ))]
            arrived(block, zs.at[t * 3 + step - 1], zr.at[t * 3 + step - 1])
            for way, goes in enumerate(ways):
                at = t * 8 + way * 4 + step
                remote_start(block, block, xs.at[at], xr.at[at], {"x": goes})

    def pass_on(t):
        ys = source(t)
        for step in range(NZ):
            bz = lax.rem(z + NZ - step, NZ)
            for way, (came, goes) in enumerate(((down, up), (up, down))):
                at = t * 8 + way * 4 + step
                arrived(spread.at[ys, :, cols(came, bz)], xs.at[at], xr.at[at])
                piece = spread.at[ys, pl.ds(way * half, half), cols(came, bz)]
                remote_start(piece, piece, fs.at[at], fr.at[at], {"x": goes})

    def complete(t):
        ys = source(t)
        for step in range(NZ):
            bz = lax.rem(z + NZ - step, NZ)
            for way in range(2):
                at = t * 8 + way * 4 + step
                arrived(spread.at[ys, pl.ds(way * half, half), cols(across, bz)], fs.at[at], fr.at[at])
        keep_own(t).wait()

    deep = 768

    def hidden(t):
        ys = source(t)
        gate_sum[...] = jnp.zeros_like(gate_sum)
        up_sum[...] = jnp.zeros_like(up_sum)
        squares[...] = jnp.zeros_like(squares)

        @pl.loop(0, D // deep)
        def _(i):
            at = pl.ds(pl.multiple_of(i * deep, 128), deep)
            piece = spread[ys, :, at]
            gate_sum[...] += jnp.dot(piece, wg[at, :], preferred_element_type=jnp.float32)
            up_sum[...] += jnp.dot(piece, wu[at, :], preferred_element_type=jnp.float32)
            wide = piece.astype(jnp.float32)
            wide = wide * wide * gain_ref[:, at]
            total = wide[:, :128]
            for lane in range(128, deep, 128):
                total = total + wide[:, lane : lane + 128]
            squares[...] += total

        tile = 48

        @pl.loop(0, rows // tile)
        def _(i):
            at = pl.ds(i * tile, tile)
            inverse = lax.rsqrt(jnp.sum(squares[at, :], axis=1, keepdims=True) / D + epsilon)
            gate = gate_sum[at, :] * inverse
            act[at, :] = (gate / (1.0 + jnp.exp(-gate)) * (up_sum[at, :] * inverse)).astype(act.dtype)

    def project(t, bx):
        ys = source(t)
        for i in range(NZ * width // deep):
            at = pl.ds(pl.multiple_of(bx * (NZ * width) + i * deep, 128), deep)
            part[ys, :, at] = jnp.dot(
                act[...], wd[:, at], preferred_element_type=jnp.float32
            ).astype(part.dtype)

    def give(t):
        ys = source(t)
        project(t, across)
        for step in range(NZ):
            for way, goes in enumerate(ways):
                at = t * 8 + way * 4 + step
                remote_start(
                    part.at[ys, pl.ds(way * half, half), cols(across, order[step])],
                    relay.at[ys, way, step],
                    rs.at[at],
                    rr.at[at],
                    {"x": goes},
                )
        for way, goes in enumerate(ways):
            project(t, goes)
            for step in range(NZ):
                at = t * 8 + way * 4 + step
                remote_start(
                    part.at[ys, pl.ds((1 - way) * half, half), cols(goes, order[step])],
                    from_x.at[ys, way, step, pl.ds((1 - way) * half, half)],
                    us.at[at],
                    ur.at[at],
                    {"x": goes},
                )
        project(t, x)

    tile = 48

    def add(dst, terms, count):
        @pl.loop(0, count // tile)
        def _(i):
            at = pl.ds(i * tile, tile)
            total = terms[0][at, :].astype(jnp.float32)
            for term in terms[1:]:
                total = total + term[at, :].astype(jnp.float32)
            dst[at, :] = total.astype(dst.dtype)

    def add_relayed(t):
        ys = source(t)
        for step in range(NZ):
            for way, goes in enumerate(ways):
                at = t * 8 + way * 4 + step
                held = relay.at[ys, way, step]
                arrived(held, rs.at[at], rr.at[at])
                add(held, (held, part.at[ys, pl.ds(way * half, half), cols(goes, order[step])]), half)
                remote_start(
                    held,
                    from_x.at[ys, way, step, pl.ds(way * half, half)],
                    vs.at[at],
                    vr.at[at],
                    {"x": goes},
                )

    def add_x(t):
        ys = source(t)
        for step in range(NZ):
            for way in range(2):
                at = t * 8 + way * 4 + step
                held = from_x.at[ys, way, step]
                arrived(held.at[pl.ds(way * half, half)], vs.at[at], vr.at[at])
                arrived(held.at[pl.ds((1 - way) * half, half)], us.at[at], ur.at[at])
            own = part.at[ys, :, cols(x, order[step])]
            add(mine.at[ys, step], (own, from_x.at[ys, 0, step], from_x.at[ys, 1, step]), rows)
            if step < NZ - 1:
                at = t * 3 + step
                remote_start(mine.at[ys, step], from_z.at[ys, step], qs.at[at], qr.at[at], {"z": order[step]})

    own_back = pltpu.make_async_copy(done.at[2 * y + w], out_ref.at[2 * y + w], back_sem)

    def add_z(t):
        ys = source(t)
        for step in range(NZ - 1):
            at = t * 3 + step
            arrived(from_z.at[ys, step], qs.at[at], qr.at[at])
        add(done.at[ys], [mine.at[ys, NZ - 1]] + [from_z.at[ys, i] for i in range(NZ - 1)], rows)

        @pl.when(t == 0)
        def _():
            own_back.start()

        @pl.when(t > 0)
        def _():
            ty, tw = place(t)
            remote_start(done.at[ys], out_ref.at[2 * y + w], os.at[t], orr.at[t], {"y": ty, "w": tw})

    begin(0)
    begin(1)

    @pl.loop(0, STEPS + 5)
    def _(t):
        def stage(offset, what):
            @pl.when((t >= offset) & (t - offset < STEPS))
            def _():
                what(t - offset)

        stage(0, along_x)

        @pl.when(t + 2 < STEPS)
        def _():
            begin(t + 2)

        stage(1, pass_on)
        stage(4, add_x)
        stage(5, add_z)

        @pl.when(t == 2)
        def _():
            for load in loads:
                load.wait()

        def first(c):
            complete(c)
            hidden(c)

        stage(2, first)
        stage(3, add_relayed)
        stage(2, give)

    own_back.wait()
    for dy, dw in others:
        j = 2 * dy + dw
        fy, fw = lax.rem(y + 4 - dy, 4), lax.rem(w + dw, 2)
        arrived(out_ref.at[2 * fy + fw], os.at[j], orr.at[j])
    for dy, dw in others:
        j = 2 * dy + dw
        left(row_ref.at[0], ds.at[j], dr.at[j])
        left(row_ref.at[0], os.at[j], orr.at[j])
        e = 2 * lax.rem(y + dy, 4) + lax.rem(w + dw, 2)
        left(pieces.at[0], ps.at[e], pr.at[e])
    left(both.at[mine_at], bs, br)
    for i in range(NZ - 1):
        left(block, azs.at[i], azr.at[i])
    for i in range(8):
        left(block, axs.at[i], axr.at[i])
        left(spot(x, z, 0), afs.at[i], afr.at[i])

    @pl.loop(0, STEPS)
    def _(t):
        for i in range(NZ - 1):
            at = t * 3 + i
            left(rows_in.at[0], zs.at[at], zr.at[at])
            left(rows_in.at[0], qs.at[at], qr.at[at])
        for i in range(8):
            at = t * 8 + i
            left(rows_in.at[0], xs.at[at], xr.at[at])
            for s, r in ((fs, fr), (rs, rr), (us, ur), (vs, vr)):
                left(rows_in.at[0, pl.ds(0, half)], s.at[at], r.at[at])


def expert_call(attended, w_out, res, own_gain, placer, gain_squares, weights, collective_id):
    kind = attended.dtype
    tokens, joined = attended.shape
    width = w_out.shape[1]
    experts = 8
    slots = placer.shape[0] // experts
    rows = slots
    hidden = 2 * weights[0].shape[1]
    any_spec, vmem_spec = pl.BlockSpec(memory_space=pl.ANY), pl.BlockSpec(memory_space=pltpu.VMEM)
    flops = 2 * STEPS * rows * D * hidden * 3
    return pl.pallas_call(
        expert_kernel,
        out_shape=(
            jax.ShapeDtypeStruct((experts, slots, width), kind),
            jax.ShapeDtypeStruct(res.shape, jnp.float32),
        ),
        in_specs=[vmem_spec] * 6 + [any_spec] * 6,
        out_specs=(vmem_spec, vmem_spec),
        scratch_shapes=[
            pltpu.VMEM((NX * NZ * tokens, joined), kind),
            pltpu.VMEM((NX, NZ * tokens, width), kind),
            pltpu.VMEM((experts, 2 * tokens, width), kind),
            pltpu.VMEM((4 * tokens, width), kind),
            pltpu.VMEM((experts, slots, width), kind),
            DMA((3,)),
            DMA((3,)),
        ]
        + [DMA((8,))] * 6
        + [DMA] * 2
        + [
            pltpu.VMEM((STEPS, rows, width), kind),
            pltpu.VMEM((STEPS, rows, D), kind),
            pltpu.VMEM((STEPS, rows, D), kind),
            pltpu.VMEM((STEPS, 2, NZ, rows // 2, width), kind),
            pltpu.VMEM((STEPS, 2, NZ, rows, width), kind),
            pltpu.VMEM((STEPS, NZ, rows, width), kind),
            pltpu.VMEM((STEPS, NZ - 1, rows, width), kind),
            pltpu.VMEM((STEPS, rows, width), kind),
            pltpu.VMEM((D, hidden), kind),
            pltpu.VMEM((D, hidden), kind),
            pltpu.VMEM((hidden, D), kind),
            pltpu.VMEM((rows, hidden), jnp.float32),
            pltpu.VMEM((rows, hidden), jnp.float32),
            pltpu.VMEM((rows, 128), jnp.float32),
            pltpu.VMEM((rows, hidden), kind),
            DMA((6,)),
            DMA((STEPS,)),
            DMA,
        ]
        + [DMA((8,))] * 2
        + [DMA((3 * STEPS,))] * 2
        + [DMA((8 * STEPS,))] * 10
        + [DMA((3 * STEPS,))] * 2
        + [DMA((8,))] * 2,
        compiler_params=pltpu.CompilerParams(
            collective_id=collective_id, has_side_effects=True, vmem_limit_bytes=60 << 20
        ),
        cost_estimate=pl.CostEstimate(flops=flops, bytes_accessed=20 << 20, transcendentals=0),
        name=f"expert_{collective_id}",
    )(attended, w_out, res, own_gain, placer, gain_squares, *weights)


def swap(array):
    return lax.ppermute(array, "k", [(0, 1), (1, 0)])


def beside(own, other, k, axis):
    return jnp.where(
        k == 0,
        jnp.concatenate([own, other], axis=axis),
        jnp.concatenate([other, own], axis=axis),
    )


def local(
    queries,
    rotated_key_cache,
    value_cache_rows,
    kv_pos,
    q_pos,
    residual,
    w_out,
    norm_gain,
    routes,
    gate_probs,
    w_gate,
    w_up,
    w_down,
):
    k = lax.axis_index("k")
    chip = lax.axis_index("x") * NZ + lax.axis_index("z")
    tokens, head_dim = queries.shape[0], rotated_key_cache.shape[1]
    heads = queries.shape[1] // head_dim
    feats = residual.shape[1]
    block_tokens = residual.shape[0]

    wg, wu, wd = w_gate[0], w_up[0], w_down[0]
    wg2, wu2, wd2 = swap(wg), swap(wu), swap(wd)
    w_out2 = beside(w_out, swap(w_out), k, 1)
    by_core = residual.reshape(2, 2, tokens, feats)
    res_own = lax.dynamic_index_in_dim(by_core, k, 1, keepdims=False).reshape(2 * tokens, feats)
    res_give = lax.dynamic_index_in_dim(by_core, 1 - k, 1, keepdims=False).reshape(2 * tokens, feats)
    res = beside(res_own, swap(res_give), k, 1)

    def by_core_rows(array):
        split = array.reshape(2, 2, tokens, array.shape[-1])
        return split.transpose(1, 0, 2, 3).reshape(block_tokens, array.shape[-1])

    experts = 8
    slots = 6 * block_tokens // experts // 2
    flat_ids = by_core_rows(routes).reshape(-1)
    probs = by_core_rows(gate_probs)
    onehot = (flat_ids[:, None] == jnp.arange(experts, dtype=jnp.int32)[None, :]).astype(jnp.int32)
    earlier = jnp.cumsum(onehot, axis=0) - onehot
    slot = jnp.sum(earlier * onehot, axis=1) - k * slots
    cell = jnp.where((slot >= 0) & (slot < slots), flat_ids * slots + slot, -1)
    cell = cell.reshape(block_tokens, 2)
    cells = jnp.arange(experts * slots, dtype=jnp.int32)
    placer = (cell[:, 0][None, :] == cells[:, None]) | (cell[:, 1][None, :] == cells[:, None])
    placer = placer.astype(jnp.bfloat16)
    layout = cell[:, :, None] == cells[None, None, :]
    picker = jnp.sum(jnp.where(layout, probs[:, :, None], 0.0), axis=1)
    picker_high = picker.astype(jnp.bfloat16)
    picker_low = (picker - picker_high.astype(jnp.float32)).astype(jnp.bfloat16)

    row_pos = jnp.tile(q_pos, heads).astype(jnp.float32)[:, None]
    gain_row = jnp.pad(norm_gain.astype(jnp.float32), (0, 2 * head_dim - feats))[None, :]
    attended, extra = attend_call(
        queries, row_pos, rotated_key_cache, value_cache_rows, kv_pos.reshape(2, 128), gain_row, 1
    )
    gains = extra[:, 1, :feats].astype(jnp.float32).reshape(1, D)
    own_gain = lax.dynamic_slice_in_dim(gains, chip * 2 * feats, 2 * feats, axis=1)

    returned, stream = expert_call(
        attended, w_out2, res, own_gain, placer, 1.0 / (gains * gains), (wg, wg2, wu, wu2, wd, wd2), 3
    )
    returned = returned.reshape(experts * slots, 2 * feats)
    mixture = jnp.dot(picker_high, returned, preferred_element_type=jnp.float32)
    mixture = mixture + jnp.dot(picker_low, returned, preferred_element_type=jnp.float32)
    here = jnp.arange(2, dtype=jnp.int32)[:, None, None] == k
    placed = jnp.where(here, stream[None], 0.0)
    share = mixture + placed.reshape(block_tokens, 2 * feats)
    keep = jnp.where(k == 0, share[:, :feats], share[:, feats:])
    give = jnp.where(k == 0, share[:, feats:], share[:, :feats])
    mixed = (keep + swap(give)).astype(jnp.bfloat16)
    mixed = mixed.reshape(2, 2, tokens, feats).transpose(1, 0, 2, 3).reshape(block_tokens, feats)
    return (attended, mixed)


def solution(mesh):
    fine = Mesh(mesh.devices.reshape(NX, NZ, 2, 4, 2), ("x", "z", "k", "y", "w"))
    ctx, exp = ("x", "z", "k"), ("y", "w")
    in_specs = (
        P(ctx, exp),
        P(ctx, exp),
        P(ctx, exp),
        P(ctx),
        P(ctx),
        P(exp, ctx),
        P(exp, ctx),
        P(ctx),
        P(exp, None),
        P(exp, None),
        P(exp, None, ctx),
        P(exp, None, ctx),
        P(exp, ctx, None),
    )
    out_specs = (P(ctx, exp), P(exp, ctx))
    return jax.shard_map(local, mesh=fine, in_specs=in_specs, out_specs=out_specs, check_vma=False)
```

```python
import jax
import jax.numpy as jnp
from jax import lax
from jax.experimental import pallas as pl
from jax.experimental.pallas import tpu as pltpu
from jax.sharding import Mesh
from jax.sharding import PartitionSpec as P

MESH = pl.DeviceIdType.MESH
DMA = pltpu.SemaphoreType.DMA
D = 6144
NX, NZ, NY = 4, 4, 4
STEPS = 8
EXPERTS = 8
neg_big = -1e30
epsilon = 1e-05
LOG2E = 1.4426950408889634

TOK, HEAD, HEADS, POS, BLOCK, SLOTS, WIDE, HID = 64, 128, 6, 256, 256, 96, 384, 512
JOINED = HEADS * HEAD
FEATS = WIDE // 2
DEEP = POS + 16

bf16, f32 = jnp.bfloat16, jnp.float32


def vmem(*shape, kind=bf16):
    return pltpu.VMEM(shape, kind)


SCRATCH = {
    "held": vmem(2 * NX * NZ, DEEP, 2 * HEAD),
    "q_rows": vmem(TOK * HEADS, HEAD),
    "limit": vmem(2 * TOK, 1, kind=f32),
    "top": vmem(TOK * HEADS, HEAD, kind=f32),
    "acc": vmem(TOK * HEADS, 2 * HEAD, kind=f32),
    "gain_squares": vmem(NX * NZ, 1, WIDE, kind=f32),
    "slab": vmem(NX * NZ * TOK, JOINED),
    "wo": vmem(WIDE, JOINED),
    "res": vmem(WIDE, BLOCK),
    "res_rows": vmem(BLOCK, WIDE),
    "leaving": vmem(NX, NZ * TOK, WIDE),
    "pieces": vmem(EXPERTS, 2 * TOK, WIDE),
    "stream": vmem(2 * TOK, WIDE, kind=f32),
    "both": vmem(BLOCK, WIDE),
    "placer": vmem(EXPERTS * SLOTS, BLOCK),
    "picker": vmem(2, BLOCK, EXPERTS * SLOTS),
    "rows_out": vmem(EXPERTS, SLOTS, WIDE),
    "rows_in": vmem(STEPS, SLOTS, WIDE),
    "spread": vmem(STEPS, NX * NZ, SLOTS, WIDE),
    "part": vmem(STEPS, NX * NZ, SLOTS, WIDE),
    "relay": vmem(STEPS, 2, NZ, SLOTS // 2, WIDE),
    "from_x": vmem(STEPS, 2, NZ, SLOTS, WIDE),
    "mine": vmem(STEPS, NZ - 1, SLOTS, WIDE),
    "from_z": vmem(STEPS, NZ - 1, SLOTS, WIDE),
    "done": vmem(STEPS, SLOTS, WIDE),
    "wg": vmem(D, HID),
    "wu": vmem(D, HID),
    "wd": vmem(HID, D),
    "gate_sum": vmem(SLOTS, HID, kind=f32),
    "up_sum": vmem(SLOTS, HID, kind=f32),
    "squares": vmem(SLOTS, 128, kind=f32),
    "act": vmem(SLOTS, HID),
    "returned": vmem(EXPERTS, SLOTS, WIDE),
    "give": vmem(BLOCK, FEATS, kind=f32),
    "got": vmem(BLOCK, FEATS, kind=f32),
    "w_sem": DMA((4,)),
    "own_sem": DMA((STEPS,)),
}
PAIRS = {
    "kz": 3, "kx": 8, "kf": 8, "kk": 12, "kh": 8,
    "az": 3, "ax": 8, "af": 8, "ap": 8, "ab": 2,
    "sw": 5, "dd": 8, "rt": 8, "ge": 1,
    "ez": 3 * STEPS, "ex": 8 * STEPS, "ef": 8 * STEPS,
    "er": 8 * STEPS, "eu": 8 * STEPS, "ev": 8 * STEPS, "eq": 3 * STEPS,
}
for pair, many in PAIRS.items():
    SCRATCH[pair + "_s"] = DMA((many,))
    SCRATCH[pair + "_r"] = DMA((many,))


def remote(src, dst, send_sem, recv_sem, device):
    return pltpu.make_async_remote_copy(
        src_ref=src,
        dst_ref=dst,
        send_sem=send_sem,
        recv_sem=recv_sem,
        device_id=device,
        device_id_type=MESH,
    )


def layer_kernel(
    q_ref, q_pos_ref, k_ref, v_ref, page_ref, gain_ref, res_ref, wo_ref, routes_ref, probs_ref,
    wg_ref, wu_ref, wd_ref, att_ref, mixed_ref, *refs,
):
    at_name = dict(zip(SCRATCH, refs))

    class R:
        pass

    for name, ref in at_name.items():
        setattr(R, name, ref)
    x, z, k, y, w = (lax.axis_index(name) for name in ("x", "z", "k", "y", "w"))
    up, down, across = lax.rem(x + 1, NX), lax.rem(x + 3, NX), lax.rem(x + 2, NX)
    ways = (up, down)
    order = [lax.rem(z + step, NZ) for step in (1, 2, 3, 0)]
    others = [(dy, dw) for dy in range(NY) for dw in range(2) if (dy, dw) != (0, 0)]
    own_expert = 2 * y + w

    def start(kind, at, src, dst, device):
        remote(src, dst, at_name[kind + "_s"].at[at], at_name[kind + "_r"].at[at], device).start()

    def arrived(kind, at, ref):
        remote(ref, ref, at_name[kind + "_s"].at[at], at_name[kind + "_r"].at[at], {"x": up}).wait_recv()

    def left(kind, at, ref):
        remote(ref, ref, at_name[kind + "_s"].at[at], at_name[kind + "_r"].at[at], {"x": up}).wait_send()

    def behind(step):
        return lax.rem(z + NZ - step, NZ)

    held = R.held
    own = 2 * (x * NZ + z) + k
    held[own, :POS, :HEAD] = k_ref[...]
    held[own, :POS, HEAD:] = v_ref[...]
    pages = page_ref[...].astype(f32) * (1.0 / 128.0)
    row = lax.broadcasted_iota(jnp.int32, (16, 2 * HEAD), 0)
    lane = lax.broadcasted_iota(jnp.int32, (16, 2 * HEAD), 1)
    numbers = jnp.where(lane == 0, pages[0:1, 0:1], jnp.where(lane == 1, pages[1:2, 0:1], 0.0))
    gain = jnp.concatenate([gain_ref[...].astype(f32), jnp.zeros((1, 2 * HEAD - FEATS), f32)], axis=1)
    extra = jnp.where(row == 0, numbers, jnp.where(row == 1, gain, 0.0))
    held[own, POS:, :] = extra.astype(bf16)

    barrier = pltpu.get_barrier_semaphore()
    peers = [{"x": up}, {"x": down}, {"k": 1 - k}]
    peers += [{"z": lax.rem(z + step, NZ)} for step in range(1, NZ)]
    peers += [{"y": lax.rem(y + dy, NY), "w": lax.rem(w + dw, 2)} for dy, dw in others]
    for device in peers:
        pl.semaphore_signal(barrier, inc=1, device_id=device, device_id_type=MESH)
    pl.semaphore_wait(barrier, len(peers))

    halves = ((0, 144), (144, DEEP - 144))

    def spot(bx, bz, core, half=None):
        where = 2 * (bx * NZ + bz) + core
        if half is None:
            return held.at[where]
        return held.at[where, pl.ds(*halves[half])]

    block = spot(x, z, k)
    for step in range(1, NZ):
        start("kz", step - 1, block, block, {"z": lax.rem(z + step, NZ)})
    for way, goes in enumerate(ways):
        start("kx", 4 * way, block, block, {"x": goes})
    start("kk", 0, block, block, {"k": 1 - k})

    def feats_of(core):
        return pl.ds(pl.multiple_of(core * FEATS, 16), FEATS)

    local_wo = pltpu.make_async_copy(wo_ref, R.wo.at[feats_of(k)], R.w_sem.at[0])
    local_wo.start()
    start("sw", 0, wo_ref, R.wo.at[feats_of(k)], {"k": 1 - k})
    R.res[feats_of(k), :] = res_ref[...]
    start("sw", 1, res_ref, R.res.at[feats_of(k)], {"k": 1 - k})

    def upright(rows):
        return jnp.concatenate([rows.astype(f32), jnp.zeros((6, BLOCK), f32)], axis=0).T

    routes = upright(routes_ref[...]).astype(jnp.int32)
    probs = upright(probs_ref[...])
    expert_lane = lax.broadcasted_iota(jnp.int32, (BLOCK, 128), 1)
    named = [(routes[:, c : c + 1] == expert_lane).astype(f32) for c in range(2)]
    before = lax.broadcasted_iota(jnp.int32, (BLOCK, BLOCK), 0) > lax.broadcasted_iota(
        jnp.int32, (BLOCK, BLOCK), 1
    )
    earlier = jnp.dot(
        before.astype(f32).astype(bf16), (named[0] + named[1]).astype(bf16), preferred_element_type=f32
    )
    slot_lane = lax.broadcasted_iota(jnp.int32, (BLOCK, EXPERTS * SLOTS), 1)
    hits = []
    for c in range(2):
        slot = jnp.sum(earlier * named[c], axis=1, keepdims=True).astype(jnp.int32) - k * SLOTS
        ok = (slot >= 0) & (slot < SLOTS)
        hits.append(jnp.where(ok, routes[:, c : c + 1] * SLOTS + slot, -1) == slot_lane)
    placer = jnp.where(hits[0], 1.0, jnp.where(hits[1], 1.0, 0.0))
    R.placer[...] = placer.T.astype(bf16)
    picker = jnp.where(hits[0], probs[:, 0:1], jnp.where(hits[1], probs[:, 1:2], 0.0))
    high = picker.astype(bf16)
    R.picker[0] = high
    R.picker[1] = (picker - high.astype(f32)).astype(bf16)

    for h in range(HEADS):
        R.q_rows[pl.ds(h * TOK, TOK), :] = q_ref[:, pl.ds(h * HEAD, HEAD)]
    R.top[...] = jnp.full_like(R.top, neg_big)
    R.acc[...] = jnp.zeros_like(R.acc)
    limit = jnp.broadcast_to(q_pos_ref[...].astype(f32), (8, TOK)).T[:, 0:1]
    R.limit[...] = jnp.concatenate([limit, limit], axis=0)
    scaling = HEAD**-0.5 * LOG2E
    tile = 2 * TOK

    def attend(bx, bz):
        where = 2 * (bx * NZ + bz)
        terms = []
        steps = lax.broadcasted_iota(jnp.int32, (1, HEAD), 1).astype(f32)
        for core in range(2):
            starts = held[where + core, POS:, :HEAD].astype(f32)
            positions = jnp.concatenate(
                [starts[0:1, 0:1] * 128.0 + steps, starts[0:1, 1:2] * 128.0 + steps], axis=1
            )
            terms.append((held[where + core, :POS, :HEAD], held[where + core, :POS, HEAD:], positions))
        ones = jnp.ones((POS, HEAD), bf16)
        limit = R.limit[...]
        for r in range(TOK * HEADS // tile):
            at = pl.ds(r * tile, tile)
            scores = []
            for keys, _, positions in terms:
                score = lax.dot_general(
                    R.q_rows[at, :], keys, (((1,), (1,)), ((), ())), preferred_element_type=f32
                )
                scores.append(jnp.where(positions <= limit, score * scaling, neg_big))
            most = jnp.maximum(scores[0], scores[1])
            most = jnp.max(jnp.maximum(most[:, :HEAD], most[:, HEAD:]), axis=1, keepdims=True)
            old = R.top[at, :]
            new = jnp.maximum(old, most)
            R.top[at, :] = new
            fade = jnp.exp2(old - new)
            total = R.acc[at, :] * jnp.concatenate([fade, fade], axis=1)
            new = jnp.concatenate([new, new], axis=1)
            for score, (_, values, _) in zip(scores, terms):
                weights = jnp.exp2(score - new).astype(bf16)
                total = total + jnp.dot(
                    weights, jnp.concatenate([values, ones], axis=1), preferred_element_type=f32
                )
            R.acc[at, :] = total

    arrived("kk", 0, spot(x, z, 1 - k))
    attend(x, z)

    @pl.loop(1, NZ)
    def _(step):
        ref = spot(x, behind(step), k)
        arrived("kz", step - 1, ref)
        for way, goes in enumerate(ways):
            start("kx", 4 * way + step, ref, ref, {"x": goes})
        start("kk", step, ref, ref, {"k": 1 - k})

    @pl.loop(0, NZ)
    def _(step):
        bz = behind(step)
        for way, (came, goes) in enumerate(((down, up), (up, down))):
            at = 4 * way + step
            ref = spot(came, bz, k)
            arrived("kx", at, ref)
            half = spot(came, bz, k, way)
            start("kf", at, half, half, {"x": goes})
            start("kk", 4 + at, ref, ref, {"k": 1 - k})

        @pl.when(step > 0)
        def _():
            arrived("kk", step, spot(x, bz, 1 - k))
            attend(x, bz)

    @pl.loop(0, NZ)
    def _(step):
        bz = behind(step)
        for way in range(2):
            at = 4 * way + step
            ref = spot(across, bz, k, way)
            arrived("kf", at, ref)
            start("kh", at, ref, ref, {"k": 1 - k})
        for way, came in enumerate((down, up)):
            arrived("kk", 4 + 4 * way + step, spot(came, bz, 1 - k))
            attend(came, bz)

    loads = [
        pltpu.make_async_copy(src, dst, R.w_sem.at[1 + i])
        for i, (src, dst) in enumerate(
            (
                (wg_ref, R.wg.at[:, pl.ds(0, HID // 2)]),
                (wu_ref, R.wu.at[:, pl.ds(0, HID // 2)]),
                (wd_ref, R.wd.at[pl.ds(0, HID // 2)]),
            )
        )
    ]
    taken = (
        (wg_ref, R.wg.at[:, pl.ds(HID // 2, HID // 2)]),
        (wu_ref, R.wu.at[:, pl.ds(HID // 2, HID // 2)]),
        (wd_ref, R.wd.at[pl.ds(HID // 2, HID // 2)]),
    )

    @pl.loop(0, NZ)
    def _(step):
        bz = behind(step)
        for way in range(2):
            arrived("kh", 4 * way + step, spot(across, bz, 1 - k, way))
        attend(across, bz)

    for i, (src, dst) in enumerate(taken):
        loads[i].start()
        start("sw", 2 + i, src, dst, {"k": 1 - k})

    slab = R.slab

    def strip(bx, bz, way=None):
        first = pl.multiple_of((bx * NZ + bz) * TOK, 16)
        if way is None:
            return slab.at[pl.ds(first, TOK)]
        return slab.at[pl.ds(pl.multiple_of(first + way * (TOK // 2), 16), TOK // 2)]

    for h in range(HEADS):
        at = pl.ds(h * TOK, TOK)
        att_ref[:, pl.ds(h * HEAD, HEAD)] = (R.acc[at, :HEAD] / R.acc[at, HEAD:]).astype(bf16)
    slab[pl.ds(pl.multiple_of((x * NZ + z) * TOK, 16), TOK), :] = att_ref[...]
    rows = strip(x, z)
    for step in range(1, NZ):
        start("az", step - 1, rows, rows, {"z": lax.rem(z + step, NZ)})
    for way, goes in enumerate(ways):
        start("ax", 4 * way, rows, rows, {"x": goes})

    for b in range(NX * NZ):
        pair = [held[2 * b + core, POS:, :].astype(f32)[1:2, :FEATS] for core in range(2)]
        gains = jnp.concatenate(pair, axis=1)
        R.gain_squares[b] = 1.0 / (gains * gains)
    local_wo.wait()
    arrived("sw", 0, R.wo.at[feats_of(1 - k)])
    arrived("sw", 1, R.res.at[feats_of(1 - k)])
    R.res_rows[...] = R.res[...].astype(f32).T.astype(bf16)

    for step in range(1, NZ):
        ref = strip(x, behind(step))
        arrived("az", step - 1, ref)
        for way, goes in enumerate(ways):
            start("ax", 4 * way + step, ref, ref, {"x": goes})

    def project_rows(bx):
        at = pl.ds(pl.multiple_of(bx * (NZ * TOK), 16), NZ * TOK)
        R.leaving[bx] = lax.dot_general(
            slab[at, :], R.wo[...], (((1,), (1,)), ((), ())), preferred_element_type=f32
        ).astype(bf16)
        for tw in range(2):
            here = (bx == y) & (tw == w)

            @pl.when(here)
            def _():
                R.pieces[own_expert] = R.leaving[bx, tw * 2 * TOK : (tw + 1) * 2 * TOK, :]

            @pl.when(jnp.logical_not(here))
            def _():
                remote(
                    R.leaving.at[bx, pl.ds(tw * 2 * TOK, 2 * TOK)],
                    R.pieces.at[own_expert],
                    R.ap_s.at[2 * bx + tw],
                    R.ap_r.at[own_expert],
                    {"y": bx, "w": tw},
                ).start()

    project_rows(x)
    for step in range(NZ):
        bz = behind(step)
        for way, (came, goes) in enumerate(((down, up), (up, down))):
            at = 4 * way + step
            arrived("ax", at, strip(came, bz))
            ref = strip(came, bz, way)
            start("af", at, ref, ref, {"x": goes})
    project_rows(up)
    project_rows(down)
    for step in range(NZ):
        bz = behind(step)
        for way in range(2):
            arrived("af", 4 * way + step, strip(across, bz, way))
    project_rows(across)

    def token_rows(core, i):
        return pl.ds(pl.multiple_of(2 * TOK * i + core * TOK, 16), TOK)

    for dy, dw in others:
        e = 2 * lax.rem(y + dy, NY) + lax.rem(w + dw, 2)
        arrived("ap", e, R.pieces.at[e])
    total = jnp.concatenate([R.res_rows[token_rows(k, i), :] for i in range(2)], axis=0).astype(f32)
    for i in range(EXPERTS):
        total = total + R.pieces[i].astype(f32)
    R.stream[...] = total
    gain_pair = [
        held[2 * (x * NZ + z) + core, POS:, :].astype(f32)[1:2, :FEATS] for core in range(2)
    ]
    scaled = (total * jnp.concatenate(gain_pair, axis=1)).astype(bf16)

    for i in range(2):
        R.both[token_rows(k, i), :] = scaled[i * TOK : (i + 1) * TOK, :]
        ref = R.both.at[token_rows(k, i)]
        start("ab", i, ref, ref, {"k": 1 - k})
    for i in range(2):
        arrived("ab", i, R.both.at[token_rows(1 - k, i)])

    def ahead(t):
        return lax.rem(t, 2) + 2 * (t // 4), lax.rem((t + 2) // 4, 2)

    def place(t):
        dy, dw = ahead(t)
        return lax.rem(y + dy, NY), lax.rem(w + dw, 2)

    def source(t):
        sy, sw = place(t)
        return 2 * sy + sw

    def place_rows(expert):
        at = pl.ds(pl.multiple_of(expert * SLOTS, 16), SLOTS)
        return jnp.dot(R.placer[at, :], R.both[...], preferred_element_type=f32).astype(bf16)

    def dispatch(t):
        dy, dw = ahead(t)
        dy = lax.rem(NY - dy, NY)
        ty, tw = lax.rem(y + dy, NY), lax.rem(w + dw, 2)
        e = 2 * ty + tw
        R.rows_out[e] = place_rows(e)
        start("dd", 2 * dy + dw, R.rows_out.at[e], R.rows_in.at[own_expert], {"y": ty, "w": tw})

    def cell(bx, bz):
        return bx * NZ + bz

    def half_of(ref, way):
        return ref.at[pl.ds(way * (SLOTS // 2), SLOTS // 2)]

    def keep_own(t):
        ys = source(t)
        return pltpu.make_async_copy(R.rows_in.at[ys], R.spread.at[ys, x * NZ + z], R.own_sem.at[t])

    def begin(t):
        ys = source(t)
        dy, dw = ahead(t)
        j = 2 * lax.rem(NY - dy, NY) + dw

        @pl.when(t > 0)
        def _():
            arrived("dd", j, R.rows_in.at[ys])

        keep_own(t).start()
        src, dst = R.rows_in.at[ys], R.spread.at[ys, x * NZ + z]
        for step in range(1, NZ):
            start("ez", t * 3 + step - 1, src, dst, {"z": lax.rem(z + step, NZ)})
        for way, goes in enumerate(ways):
            start("ex", t * 8 + way * 4, src, dst, {"x": goes})

    def along_x(t):
        ys = source(t)
        for step in range(1, NZ):
            ref = R.spread.at[ys, cell(x, behind(step))]
            arrived("ez", t * 3 + step - 1, ref)
            for way, goes in enumerate(ways):
                start("ex", t * 8 + way * 4 + step, ref, ref, {"x": goes})

    def pass_on(t):
        ys = source(t)
        for step in range(NZ):
            for way, (came, goes) in enumerate(((down, up), (up, down))):
                at = t * 8 + way * 4 + step
                ref = R.spread.at[ys, cell(came, behind(step))]
                arrived("ex", at, ref)
                start("ef", at, half_of(ref, way), half_of(ref, way), {"x": goes})

    def complete(t):
        ys = source(t)
        for step in range(NZ):
            for way in range(2):
                ref = R.spread.at[ys, cell(across, behind(step))]
                arrived("ef", t * 8 + way * 4 + step, half_of(ref, way))
        keep_own(t).wait()

    deep = 2 * WIDE

    def hidden(t):
        ys = source(t)
        R.gate_sum[...] = jnp.zeros_like(R.gate_sum)
        R.up_sum[...] = jnp.zeros_like(R.up_sum)
        R.squares[...] = jnp.zeros_like(R.squares)

        @pl.loop(0, D // deep)
        def _(i):
            at = pl.ds(pl.multiple_of(i * deep, 128), deep)
            piece = jnp.concatenate([R.spread[ys, 2 * i], R.spread[ys, 2 * i + 1]], axis=1)
            R.gate_sum[...] += jnp.dot(piece, R.wg[at, :], preferred_element_type=f32)
            R.up_sum[...] += jnp.dot(piece, R.wu[at, :], preferred_element_type=f32)
            wide = piece.astype(f32)
            wide = wide * wide
            wide = wide * jnp.concatenate([R.gain_squares[2 * i], R.gain_squares[2 * i + 1]], axis=1)
            total = wide[:, :128]
            for lane in range(128, deep, 128):
                total = total + wide[:, lane : lane + 128]
            R.squares[...] += total

        tile = 48

        @pl.loop(0, SLOTS // tile)
        def _(i):
            at = pl.ds(i * tile, tile)
            inverse = lax.rsqrt(jnp.sum(R.squares[at, :], axis=1, keepdims=True) / D + epsilon)
            gate = R.gate_sum[at, :] * inverse
            R.act[at, :] = (gate / (1.0 + jnp.exp(-gate)) * (R.up_sum[at, :] * inverse)).astype(bf16)

    def project(t, bx):
        ys = source(t)
        for i in range(NZ // 2):
            at = pl.ds(pl.multiple_of(bx * (NZ * WIDE) + i * deep, 128), deep)
            term = jnp.dot(R.act[...], R.wd[:, at], preferred_element_type=f32).astype(bf16)
            R.part[ys, cell(bx, 2 * i)] = term[:, :WIDE]
            R.part[ys, cell(bx, 2 * i + 1)] = term[:, WIDE:]

    def hand_out(t):
        ys = source(t)
        project(t, across)
        for step in range(NZ):
            for way, goes in enumerate(ways):
                ref = half_of(R.part.at[ys, cell(across, order[step])], way)
                start("er", t * 8 + way * 4 + step, ref, R.relay.at[ys, way, step], {"x": goes})
        for way, goes in enumerate(ways):
            project(t, goes)
            for step in range(NZ):
                ref = half_of(R.part.at[ys, cell(goes, order[step])], 1 - way)
                dst = half_of(R.from_x.at[ys, way, step], 1 - way)
                start("eu", t * 8 + way * 4 + step, ref, dst, {"x": goes})
        project(t, x)

    def add(dst, terms, count):
        tile = 48

        @pl.loop(0, count // tile)
        def _(i):
            at = pl.ds(i * tile, tile)
            total = terms[0][at, :].astype(f32)
            for term in terms[1:]:
                total = total + term[at, :].astype(f32)
            dst[at, :] = total.astype(dst.dtype)

    def add_relayed(t):
        ys = source(t)
        for step in range(NZ):
            for way, goes in enumerate(ways):
                at = t * 8 + way * 4 + step
                ref = R.relay.at[ys, way, step]
                arrived("er", at, ref)
                add(ref, (ref, half_of(R.part.at[ys, cell(goes, order[step])], way)), SLOTS // 2)
                start("ev", at, ref, half_of(R.from_x.at[ys, way, step], way), {"x": goes})

    def x_terms(ys, step):
        own = R.part.at[ys, cell(x, order[step])]
        return [own, R.from_x.at[ys, 0, step], R.from_x.at[ys, 1, step]]

    def add_x(t):
        ys = source(t)
        for step in range(NZ):
            for way in range(2):
                at = t * 8 + way * 4 + step
                ref = R.from_x.at[ys, way, step]
                arrived("ev", at, half_of(ref, way))
                arrived("eu", at, half_of(ref, 1 - way))
            if step < NZ - 1:
                mine = R.mine.at[ys, step]
                add(mine, x_terms(ys, step), SLOTS)
                start("eq", t * 3 + step, mine, R.from_z.at[ys, step], {"z": order[step]})

    def add_z(t):
        ys = source(t)
        for step in range(NZ - 1):
            arrived("eq", t * 3 + step, R.from_z.at[ys, step])
        terms = x_terms(ys, NZ - 1) + [R.from_z.at[ys, i] for i in range(NZ - 1)]

        @pl.when(t == 0)
        def _():
            add(R.returned.at[own_expert], terms, SLOTS)

        @pl.when(t > 0)
        def _():
            add(R.done.at[ys], terms, SLOTS)
            dy, dw = ahead(t)
            ty, tw = place(t)
            start("rt", 2 * dy + dw, R.done.at[ys], R.returned.at[own_expert], {"y": ty, "w": tw})

    R.rows_in[own_expert] = place_rows(own_expert)
    begin(0)
    dispatch(1)
    dispatch(2)
    dispatch(3)
    begin(1)

    @pl.loop(0, STEPS + 5)
    def _(t):
        def stage(offset, what):
            @pl.when((t >= offset) & (t - offset < STEPS))
            def _():
                what(t - offset)

        stage(0, along_x)

        @pl.when(t + 4 < STEPS)
        def _():
            dispatch(t + 4)

        @pl.when(t + 2 < STEPS)
        def _():
            begin(t + 2)

        stage(1, pass_on)
        stage(4, add_x)
        stage(5, add_z)

        @pl.when(t == 2)
        def _():
            for i, (src, dst) in enumerate(taken):
                loads[i].wait()
                arrived("sw", 2 + i, dst)

        def first(c):
            complete(c)
            hidden(c)

        stage(2, first)
        stage(3, add_relayed)
        stage(2, hand_out)

    for dy, dw in others:
        fy, fw = lax.rem(y + NY - dy, NY), lax.rem(w + dw, 2)
        arrived("rt", 2 * dy + dw, R.returned.at[2 * fy + fw])
    results = R.returned[...].reshape(EXPERTS * SLOTS, WIDE)
    share = jnp.dot(R.picker[0], results, preferred_element_type=f32)
    share = share + jnp.dot(R.picker[1], results, preferred_element_type=f32)
    zero = jnp.zeros((TOK, WIDE), f32)
    parts = []
    for i in range(2):
        mine = R.stream[i * TOK : (i + 1) * TOK, :]
        parts += [jnp.where(k == 0, mine, zero), jnp.where(k == 0, zero, mine)]
    share = share + jnp.concatenate(parts, axis=0)
    first, second = share[:, :FEATS], share[:, FEATS:]
    R.give[...] = jnp.where(k == 0, second, first)
    start("ge", 0, R.give, R.got, {"k": 1 - k})
    keep = jnp.where(k == 0, first, second)
    arrived("ge", 0, R.got)
    mixed_ref[...] = (keep + R.got[...]).T.astype(bf16)

    left("ge", 0, R.give)
    for i in range(NZ - 1):
        left("kz", i, block)
        left("az", i, rows)
    for i in range(12):
        left("kk", i, block)
    for i in range(8):
        left("kx", i, block)
        left("kf", i, spot(x, z, k, i // 4))
        left("kh", i, spot(x, z, k, i // 4))
        left("ax", i, rows)
        left("af", i, strip(x, z, 0))
    for i in range(2):
        left("ab", i, R.both.at[pl.ds(0, TOK)])
    left("sw", 0, R.wo.at[feats_of(0)])
    left("sw", 1, R.res.at[feats_of(0)])
    for i, (src, dst) in enumerate(taken):
        left("sw", 2 + i, dst)
    for dy, dw in others:
        e = 2 * lax.rem(y + dy, NY) + lax.rem(w + dw, 2)
        left("ap", e, R.pieces.at[0])
        left("dd", 2 * dy + dw, R.rows_in.at[0])
        left("rt", 2 * dy + dw, R.rows_in.at[0])

    @pl.loop(0, STEPS)
    def _(t):
        for i in range(NZ - 1):
            left("ez", t * 3 + i, R.rows_in.at[0])
            left("eq", t * 3 + i, R.rows_in.at[0])
        for i in range(8):
            left("ex", t * 8 + i, R.rows_in.at[0])
            for kind in ("ef", "er", "eu", "ev"):
                left(kind, t * 8 + i, half_of(R.rows_in.at[0], 0))


def local(
    queries,
    rotated_key_cache,
    value_cache_rows,
    kv_pos,
    q_pos,
    residual,
    w_out,
    norm_gain,
    routes,
    gate_probs,
    w_gate,
    w_up,
    w_down,
):
    any_spec, vmem_spec = pl.BlockSpec(memory_space=pl.ANY), pl.BlockSpec(memory_space=pltpu.VMEM)
    flops = 2 * STEPS * SLOTS * D * HID * 3
    attended, mixed = pl.pallas_call(
        layer_kernel,
        out_shape=(
            jax.ShapeDtypeStruct((TOK, JOINED), bf16),
            jax.ShapeDtypeStruct((FEATS, BLOCK), bf16),
        ),
        in_specs=[vmem_spec] * 7 + [any_spec] + [vmem_spec] * 2 + [any_spec] * 3,
        out_specs=(vmem_spec, vmem_spec),
        scratch_shapes=list(SCRATCH.values()),
        compiler_params=pltpu.CompilerParams(
            collective_id=1, has_side_effects=True, vmem_limit_bytes=63 << 20
        ),
        cost_estimate=pl.CostEstimate(flops=flops, bytes_accessed=20 << 20, transcendentals=0),
        name="layer",
    )(
        queries,
        q_pos[None, :],
        rotated_key_cache,
        value_cache_rows,
        kv_pos.reshape(2, 128),
        norm_gain[None, :],
        residual.T,
        w_out.T,
        routes.T,
        gate_probs.T,
        w_gate[0],
        w_up[0],
        w_down[0],
    )
    return attended, mixed.T


def solution(mesh):
    fine = Mesh(mesh.devices.reshape(NX, NZ, 2, 4, 2), ("x", "z", "k", "y", "w"))
    ctx, exp = ("x", "z", "k"), ("y", "w")
    in_specs = (
        P(ctx, exp),
        P(ctx, exp),
        P(ctx, exp),
        P(ctx),
        P(ctx),
        P(exp, ctx),
        P(exp, ctx),
        P(ctx),
        P(exp, None),
        P(exp, None),
        P(exp, None, ctx),
        P(exp, None, ctx),
        P(exp, ctx, None),
    )
    out_specs = (P(ctx, exp), P(exp, ctx))
    return jax.shard_map(local, mesh=fine, in_specs=in_specs, out_specs=out_specs, check_vma=False)
```

```python
import jax
import jax.numpy as jnp
from jax import lax
from jax.experimental import pallas as pl
from jax.experimental.pallas import tpu as pltpu
from jax.sharding import Mesh
from jax.sharding import PartitionSpec as P

MESH = pl.DeviceIdType.MESH
DMA = pltpu.SemaphoreType.DMA
D = 6144
NX, NZ, NY = 4, 4, 4
STEPS = 8
EXPERTS = 8
neg_big = -1e30
epsilon = 1e-05
LOG2E = 1.4426950408889634

TOK, HEAD, HEADS, POS, BLOCK, SLOTS, WIDE, HID = 64, 128, 6, 256, 256, 96, 384, 512
JOINED = HEADS * HEAD
FEATS = WIDE // 2
DEEP = POS + 16

bf16, f32 = jnp.bfloat16, jnp.float32


def vmem(*shape, kind=bf16):
    return pltpu.VMEM(shape, kind)


SCRATCH = {
    "held": vmem(2 * NX * NZ, DEEP, 2 * HEAD),
    "q_rows": vmem(TOK * HEADS, HEAD),
    "limit": vmem(2 * TOK, 1, kind=f32),
    "top": vmem(TOK * HEADS, HEAD, kind=f32),
    "acc": vmem(TOK * HEADS, 2 * HEAD, kind=f32),
    "gain_squares": vmem(NX * NZ, 1, WIDE, kind=f32),
    "slab": vmem(NX * NZ * TOK, JOINED),
    "wo": vmem(WIDE, JOINED),
    "res": vmem(WIDE, BLOCK),
    "res_rows": vmem(BLOCK, WIDE),
    "leaving": vmem(NX, NZ * TOK, WIDE),
    "pieces": vmem(EXPERTS, 2 * TOK, WIDE),
    "stream": vmem(2 * TOK, WIDE, kind=f32),
    "both": vmem(BLOCK, WIDE),
    "placer": vmem(EXPERTS * SLOTS, BLOCK),
    "picker": vmem(2, BLOCK, EXPERTS * SLOTS),
    "rows_out": vmem(EXPERTS, SLOTS, WIDE),
    "rows_in": vmem(STEPS, SLOTS, WIDE),
    "spread": vmem(STEPS, NX * NZ, SLOTS, WIDE),
    "part": vmem(STEPS, NX * NZ, SLOTS, WIDE),
    "relay": vmem(STEPS, 2, NZ, SLOTS // 2, WIDE),
    "from_x": vmem(STEPS, 2, NZ, SLOTS, WIDE),
    "mine": vmem(STEPS, NZ - 1, SLOTS, WIDE),
    "from_z": vmem(STEPS, NZ - 1, SLOTS, WIDE),
    "done": vmem(STEPS, SLOTS, WIDE),
    "wg": vmem(D, HID),
    "wu": vmem(D, HID),
    "wd": vmem(HID, D),
    "gate_sum": vmem(SLOTS, HID, kind=f32),
    "up_sum": vmem(SLOTS, HID, kind=f32),
    "squares": vmem(SLOTS, 128, kind=f32),
    "act": vmem(SLOTS, HID),
    "returned": vmem(EXPERTS, SLOTS, WIDE),
    "give": vmem(BLOCK, FEATS, kind=f32),
    "got": vmem(BLOCK, FEATS, kind=f32),
    "w_sem": DMA((4,)),
    "own_sem": DMA((STEPS,)),
}
KINDS = {
    "kz": 3, "kx": 4, "kf": 4, "kk": 8, "kh": 4,
    "az": 3, "ax": 4, "af": 1, "ap": 1, "ab": 1,
    "dd": 8, "rt": 1, "ge": 1, "two": 1, "tre": 1, "twg": 1, "twu": 1, "twd": 1,
    "ez": 3 * STEPS, "ex": 4 * STEPS, "ef": STEPS,
    "er": 4 * STEPS, "eu": STEPS, "ev": 4 * STEPS, "eq": STEPS,
}
SCRATCH["sent"] = DMA((len(KINDS),))
for kind, many in KINDS.items():
    SCRATCH[kind] = DMA((many,))


def remote(src, dst, send_sem, recv_sem, device):
    return pltpu.make_async_remote_copy(
        src_ref=src,
        dst_ref=dst,
        send_sem=send_sem,
        recv_sem=recv_sem,
        device_id=device,
        device_id_type=MESH,
    )


def layer_kernel(
    q_ref, q_pos_ref, k_ref, v_ref, page_ref, gain_ref, res_ref, wo_ref, routes_ref, probs_ref,
    wg_ref, wu_ref, wd_ref, att_ref, mixed_ref, *refs,
):
    at_name = dict(zip(SCRATCH, refs))

    class R:
        pass

    for name, ref in at_name.items():
        setattr(R, name, ref)
    x, z, k, y, w = (lax.axis_index(name) for name in ("x", "z", "k", "y", "w"))
    up, down, across = lax.rem(x + 1, NX), lax.rem(x + 3, NX), lax.rem(x + 2, NX)
    ways = (up, down)
    order = [lax.rem(z + step, NZ) for step in (1, 2, 3, 0)]
    others = [(dy, dw) for dy in range(NY) for dw in range(2) if (dy, dw) != (0, 0)]
    own_expert = 2 * y + w

    kinds = list(KINDS)

    def start(kind, at, src, dst, device):
        remote(src, dst, R.sent.at[kinds.index(kind)], at_name[kind].at[at], device).start()

    def arrived(kind, at, ref):
        remote(ref, ref, R.sent.at[kinds.index(kind)], at_name[kind].at[at], {"x": up}).wait_recv()

    def left(kind, ref):
        remote(ref, ref, R.sent.at[kinds.index(kind)], at_name[kind].at[0], {"x": up}).wait_send()

    def behind(step):
        return lax.rem(z + NZ - step, NZ)

    held = R.held
    own = 2 * (x * NZ + z) + k
    held[own, :POS, :HEAD] = k_ref[...]
    held[own, :POS, HEAD:] = v_ref[...]
    pages = page_ref[...].astype(f32) * (1.0 / 128.0)
    row = lax.broadcasted_iota(jnp.int32, (16, 2 * HEAD), 0)
    lane = lax.broadcasted_iota(jnp.int32, (16, 2 * HEAD), 1)
    numbers = jnp.where(lane == 0, pages[0:1, 0:1], jnp.where(lane == 1, pages[1:2, 0:1], 0.0))
    gain = jnp.concatenate([gain_ref[...].astype(f32), jnp.zeros((1, 2 * HEAD - FEATS), f32)], axis=1)
    extra = jnp.where(row == 0, numbers, jnp.where(row == 1, gain, 0.0))
    held[own, POS:, :] = extra.astype(bf16)

    barrier = pltpu.get_barrier_semaphore()
    peers = [{"x": up}, {"x": down}, {"k": 1 - k}]
    peers += [{"z": lax.rem(z + step, NZ)} for step in range(1, NZ)]
    peers += [{"y": lax.rem(y + dy, NY), "w": lax.rem(w + dw, 2)} for dy, dw in others]
    for device in peers:
        pl.semaphore_signal(barrier, inc=1, device_id=device, device_id_type=MESH)
    pl.semaphore_wait(barrier, len(peers))

    halves = ((0, 144), (144, DEEP - 144))

    def spot(bx, bz, core, half=None):
        where = 2 * (bx * NZ + bz) + core
        if half is None:
            return held.at[where]
        return held.at[where, pl.ds(*halves[half])]

    block = spot(x, z, k)
    for step in range(1, NZ):
        start("kz", step - 1, block, block, {"z": lax.rem(z + step, NZ)})
    for way, goes in enumerate(ways):
        start("kx", 0, block, block, {"x": goes})
    start("kk", 0, block, block, {"k": 1 - k})

    def feats_of(core):
        return pl.ds(pl.multiple_of(core * FEATS, 16), FEATS)

    local_wo = pltpu.make_async_copy(wo_ref, R.wo.at[feats_of(k)], R.w_sem.at[0])
    local_wo.start()
    start("two", 0, wo_ref, R.wo.at[feats_of(k)], {"k": 1 - k})
    R.res[feats_of(k), :] = res_ref[...]
    start("tre", 0, res_ref, R.res.at[feats_of(k)], {"k": 1 - k})

    def upright(rows):
        return jnp.concatenate([rows.astype(f32), jnp.zeros((6, BLOCK), f32)], axis=0).T

    routes = upright(routes_ref[...]).astype(jnp.int32)
    probs = upright(probs_ref[...])
    expert_lane = lax.broadcasted_iota(jnp.int32, (BLOCK, 128), 1)
    named = [(routes[:, c : c + 1] == expert_lane).astype(f32) for c in range(2)]
    before = lax.broadcasted_iota(jnp.int32, (BLOCK, BLOCK), 0) > lax.broadcasted_iota(
        jnp.int32, (BLOCK, BLOCK), 1
    )
    earlier = jnp.dot(
        before.astype(f32).astype(bf16), (named[0] + named[1]).astype(bf16), preferred_element_type=f32
    )
    slot_lane = lax.broadcasted_iota(jnp.int32, (BLOCK, EXPERTS * SLOTS), 1)
    hits = []
    for c in range(2):
        slot = jnp.sum(earlier * named[c], axis=1, keepdims=True).astype(jnp.int32) - k * SLOTS
        ok = (slot >= 0) & (slot < SLOTS)
        hits.append(jnp.where(ok, routes[:, c : c + 1] * SLOTS + slot, -1) == slot_lane)
    placer = jnp.where(hits[0], 1.0, jnp.where(hits[1], 1.0, 0.0))
    R.placer[...] = placer.T.astype(bf16)
    picker = jnp.where(hits[0], probs[:, 0:1], jnp.where(hits[1], probs[:, 1:2], 0.0))
    high = picker.astype(bf16)
    R.picker[0] = high
    R.picker[1] = (picker - high.astype(f32)).astype(bf16)

    for h in range(HEADS):
        R.q_rows[pl.ds(h * TOK, TOK), :] = q_ref[:, pl.ds(h * HEAD, HEAD)]
    R.top[...] = jnp.full_like(R.top, neg_big)
    R.acc[...] = jnp.zeros_like(R.acc)
    limit = jnp.broadcast_to(q_pos_ref[...].astype(f32), (8, TOK)).T[:, 0:1]
    R.limit[...] = jnp.concatenate([limit, limit], axis=0)
    scaling = HEAD**-0.5 * LOG2E
    tile = 2 * TOK

    def attend(bx, bz):
        where = 2 * (bx * NZ + bz)
        terms = []
        steps = lax.broadcasted_iota(jnp.int32, (1, HEAD), 1).astype(f32)
        for core in range(2):
            starts = held[where + core, POS:, :HEAD].astype(f32)
            positions = jnp.concatenate(
                [starts[0:1, 0:1] * 128.0 + steps, starts[0:1, 1:2] * 128.0 + steps], axis=1
            )
            terms.append((held[where + core, :POS, :HEAD], held[where + core, :POS, HEAD:], positions))
        ones = jnp.ones((POS, HEAD), bf16)
        limit = R.limit[...]
        for r in range(TOK * HEADS // tile):
            at = pl.ds(r * tile, tile)
            scores = []
            for keys, _, positions in terms:
                score = lax.dot_general(
                    R.q_rows[at, :], keys, (((1,), (1,)), ((), ())), preferred_element_type=f32
                )
                scores.append(jnp.where(positions <= limit, score * scaling, neg_big))
            most = jnp.maximum(scores[0], scores[1])
            most = jnp.max(jnp.maximum(most[:, :HEAD], most[:, HEAD:]), axis=1, keepdims=True)
            old = R.top[at, :]
            new = jnp.maximum(old, most)
            R.top[at, :] = new
            fade = jnp.exp2(old - new)
            total = R.acc[at, :] * jnp.concatenate([fade, fade], axis=1)
            new = jnp.concatenate([new, new], axis=1)
            for score, (_, values, _) in zip(scores, terms):
                weights = jnp.exp2(score - new).astype(bf16)
                total = total + jnp.dot(
                    weights, jnp.concatenate([values, ones], axis=1), preferred_element_type=f32
                )
            R.acc[at, :] = total

    arrived("kk", 0, spot(x, z, 1 - k))
    attend(x, z)

    @pl.loop(1, NZ)
    def _(step):
        ref = spot(x, behind(step), k)
        arrived("kz", step - 1, ref)
        for way, goes in enumerate(ways):
            start("kx", step, ref, ref, {"x": goes})
        start("kk", step, ref, ref, {"k": 1 - k})

    @pl.loop(0, NZ)
    def _(step):
        bz = behind(step)
        arrived("kx", step, held.at[pl.ds(0, 2)])
        for way, (came, goes) in enumerate(((down, up), (up, down))):
            ref = spot(came, bz, k)
            half = spot(came, bz, k, way)
            start("kf", step, half, half, {"x": goes})
            start("kk", NZ + step, ref, ref, {"k": 1 - k})

        @pl.when(step > 0)
        def _():
            arrived("kk", step, spot(x, bz, 1 - k))
            attend(x, bz)

    @pl.loop(0, NZ)
    def _(step):
        bz = behind(step)
        ref = spot(across, bz, k)
        arrived("kf", step, ref)
        start("kh", step, ref, ref, {"k": 1 - k})
        arrived("kk", NZ + step, held.at[pl.ds(0, 2)])
        for came in (down, up):
            attend(came, bz)

    loads = [
        pltpu.make_async_copy(src, dst, R.w_sem.at[1 + i])
        for i, (src, dst) in enumerate(
            (
                (wg_ref, R.wg.at[:, pl.ds(0, HID // 2)]),
                (wu_ref, R.wu.at[:, pl.ds(0, HID // 2)]),
                (wd_ref, R.wd.at[pl.ds(0, HID // 2)]),
            )
        )
    ]
    taken = (
        (wg_ref, R.wg.at[:, pl.ds(HID // 2, HID // 2)]),
        (wu_ref, R.wu.at[:, pl.ds(HID // 2, HID // 2)]),
        (wd_ref, R.wd.at[pl.ds(HID // 2, HID // 2)]),
    )

    @pl.loop(0, NZ)
    def _(step):
        bz = behind(step)
        arrived("kh", step, spot(across, bz, 1 - k))
        attend(across, bz)

    for i, (src, dst) in enumerate(taken):
        loads[i].start()
        start(("twg", "twu", "twd")[i], 0, src, dst, {"k": 1 - k})

    slab = R.slab

    def strip(bx, bz, way=None):
        first = pl.multiple_of((bx * NZ + bz) * TOK, 16)
        if way is None:
            return slab.at[pl.ds(first, TOK)]
        return slab.at[pl.ds(pl.multiple_of(first + way * (TOK // 2), 16), TOK // 2)]

    for h in range(HEADS):
        at = pl.ds(h * TOK, TOK)
        att_ref[:, pl.ds(h * HEAD, HEAD)] = (R.acc[at, :HEAD] / R.acc[at, HEAD:]).astype(bf16)
    slab[pl.ds(pl.multiple_of((x * NZ + z) * TOK, 16), TOK), :] = att_ref[...]
    rows = strip(x, z)
    for step in range(1, NZ):
        start("az", step - 1, rows, rows, {"z": lax.rem(z + step, NZ)})
    for way, goes in enumerate(ways):
        start("ax", 0, rows, rows, {"x": goes})

    for b in range(NX * NZ):
        pair = [held[2 * b + core, POS:, :].astype(f32)[1:2, :FEATS] for core in range(2)]
        gains = jnp.concatenate(pair, axis=1)
        R.gain_squares[b] = 1.0 / (gains * gains)
    local_wo.wait()
    arrived("two", 0, R.wo.at[feats_of(1 - k)])
    arrived("tre", 0, R.res.at[feats_of(1 - k)])
    R.res_rows[...] = R.res[...].astype(f32).T.astype(bf16)

    for step in range(1, NZ):
        ref = strip(x, behind(step))
        arrived("az", step - 1, ref)
        for way, goes in enumerate(ways):
            start("ax", step, ref, ref, {"x": goes})

    def project_rows(bx):
        at = pl.ds(pl.multiple_of(bx * (NZ * TOK), 16), NZ * TOK)
        R.leaving[bx] = lax.dot_general(
            slab[at, :], R.wo[...], (((1,), (1,)), ((), ())), preferred_element_type=f32
        ).astype(bf16)
        for tw in range(2):
            here = (bx == y) & (tw == w)

            @pl.when(here)
            def _():
                R.pieces[own_expert] = R.leaving[bx, tw * 2 * TOK : (tw + 1) * 2 * TOK, :]

            @pl.when(jnp.logical_not(here))
            def _():
                piece = R.leaving.at[bx, pl.ds(tw * 2 * TOK, 2 * TOK)]
                start("ap", 0, piece, R.pieces.at[own_expert], {"y": bx, "w": tw})

    project_rows(x)
    for step in range(NZ):
        bz = behind(step)
        arrived("ax", step, slab.at[pl.ds(0, 2 * TOK)])
        for way, (came, goes) in enumerate(((down, up), (up, down))):
            ref = strip(came, bz, way)
            start("af", 0, ref, ref, {"x": goes})
    project_rows(up)
    project_rows(down)
    arrived("af", 0, slab.at[pl.ds(0, NZ * TOK)])
    project_rows(across)

    def token_rows(core, i):
        return pl.ds(pl.multiple_of(2 * TOK * i + core * TOK, 16), TOK)

    arrived("ap", 0, R.pieces.at[pl.ds(0, EXPERTS - 1)])
    total = jnp.concatenate([R.res_rows[token_rows(k, i), :] for i in range(2)], axis=0).astype(f32)
    for i in range(EXPERTS):
        total = total + R.pieces[i].astype(f32)
    R.stream[...] = total
    gain_pair = [
        held[2 * (x * NZ + z) + core, POS:, :].astype(f32)[1:2, :FEATS] for core in range(2)
    ]
    scaled = (total * jnp.concatenate(gain_pair, axis=1)).astype(bf16)

    for i in range(2):
        R.both[token_rows(k, i), :] = scaled[i * TOK : (i + 1) * TOK, :]
        ref = R.both.at[token_rows(k, i)]
        start("ab", 0, ref, ref, {"k": 1 - k})
    arrived("ab", 0, R.both.at[pl.ds(0, 2 * TOK)])

    def ahead(t):
        return lax.rem(t, 2) + 2 * (t // 4), lax.rem((t + 2) // 4, 2)

    def place(t):
        dy, dw = ahead(t)
        return lax.rem(y + dy, NY), lax.rem(w + dw, 2)

    def source(t):
        sy, sw = place(t)
        return 2 * sy + sw

    def place_rows(expert):
        at = pl.ds(pl.multiple_of(expert * SLOTS, 16), SLOTS)
        return jnp.dot(R.placer[at, :], R.both[...], preferred_element_type=f32).astype(bf16)

    def dispatch(t):
        dy, dw = ahead(t)
        dy = lax.rem(NY - dy, NY)
        ty, tw = lax.rem(y + dy, NY), lax.rem(w + dw, 2)
        e = 2 * ty + tw
        R.rows_out[e] = place_rows(e)
        start("dd", 2 * dy + dw, R.rows_out.at[e], R.rows_in.at[own_expert], {"y": ty, "w": tw})

    def cell(bx, bz):
        return bx * NZ + bz

    def half_of(ref, way):
        return ref.at[pl.ds(way * (SLOTS // 2), SLOTS // 2)]

    def keep_own(t):
        ys = source(t)
        return pltpu.make_async_copy(R.rows_in.at[ys], R.spread.at[ys, x * NZ + z], R.own_sem.at[t])

    def begin(t):
        ys = source(t)
        dy, dw = ahead(t)
        j = 2 * lax.rem(NY - dy, NY) + dw

        @pl.when(t > 0)
        def _():
            arrived("dd", j, R.rows_in.at[ys])

        keep_own(t).start()
        src, dst = R.rows_in.at[ys], R.spread.at[ys, x * NZ + z]
        for step in range(1, NZ):
            start("ez", t * 3 + step - 1, src, dst, {"z": lax.rem(z + step, NZ)})
        for way, goes in enumerate(ways):
            start("ex", t * 4, src, dst, {"x": goes})

    def along_x(t):
        ys = source(t)
        for step in range(1, NZ):
            ref = R.spread.at[ys, cell(x, behind(step))]
            arrived("ez", t * 3 + step - 1, ref)
            for way, goes in enumerate(ways):
                start("ex", t * 4 + step, ref, ref, {"x": goes})

    def pass_on(t):
        ys = source(t)
        for step in range(NZ):
            arrived("ex", t * 4 + step, R.from_x.at[ys, 0, pl.ds(0, 2)])
            for way, (came, goes) in enumerate(((down, up), (up, down))):
                ref = half_of(R.spread.at[ys, cell(came, behind(step))], way)
                start("ef", t, ref, ref, {"x": goes})

    def complete(t):
        ys = source(t)
        arrived("ef", t, R.spread.at[ys, pl.ds(across * NZ, NZ)])
        keep_own(t).wait()

    deep = 2 * WIDE

    def hidden(t):
        ys = source(t)
        R.gate_sum[...] = jnp.zeros_like(R.gate_sum)
        R.up_sum[...] = jnp.zeros_like(R.up_sum)
        R.squares[...] = jnp.zeros_like(R.squares)

        @pl.loop(0, D // deep)
        def _(i):
            at = pl.ds(pl.multiple_of(i * deep, 128), deep)
            piece = jnp.concatenate([R.spread[ys, 2 * i], R.spread[ys, 2 * i + 1]], axis=1)
            R.gate_sum[...] += jnp.dot(piece, R.wg[at, :], preferred_element_type=f32)
            R.up_sum[...] += jnp.dot(piece, R.wu[at, :], preferred_element_type=f32)
            wide = piece.astype(f32)
            wide = wide * wide
            wide = wide * jnp.concatenate([R.gain_squares[2 * i], R.gain_squares[2 * i + 1]], axis=1)
            total = wide[:, :128]
            for lane in range(128, deep, 128):
                total = total + wide[:, lane : lane + 128]
            R.squares[...] += total

        tile = 48

        @pl.loop(0, SLOTS // tile)
        def _(i):
            at = pl.ds(i * tile, tile)
            inverse = lax.rsqrt(jnp.sum(R.squares[at, :], axis=1, keepdims=True) / D + epsilon)
            gate = R.gate_sum[at, :] * inverse
            R.act[at, :] = (gate / (1.0 + jnp.exp(-gate)) * (R.up_sum[at, :] * inverse)).astype(bf16)

    def project(t, bx):
        ys = source(t)
        for i in range(NZ // 2):
            at = pl.ds(pl.multiple_of(bx * (NZ * WIDE) + i * deep, 128), deep)
            term = jnp.dot(R.act[...], R.wd[:, at], preferred_element_type=f32).astype(bf16)
            R.part[ys, cell(bx, 2 * i)] = term[:, :WIDE]
            R.part[ys, cell(bx, 2 * i + 1)] = term[:, WIDE:]

    def hand_out(t):
        ys = source(t)
        project(t, across)
        for step in range(NZ):
            for way, goes in enumerate(ways):
                ref = half_of(R.part.at[ys, cell(across, order[step])], way)
                start("er", t * 4 + step, ref, R.relay.at[ys, way, step], {"x": goes})
        for way, goes in enumerate(ways):
            project(t, goes)
            for step in range(NZ):
                ref = half_of(R.part.at[ys, cell(goes, order[step])], 1 - way)
                dst = half_of(R.from_x.at[ys, way, step], 1 - way)
                start("eu", t, ref, dst, {"x": goes})
        project(t, x)

    def add(dst, terms, count):
        tile = 48

        @pl.loop(0, count // tile)
        def _(i):
            at = pl.ds(i * tile, tile)
            total = terms[0][at, :].astype(f32)
            for term in terms[1:]:
                total = total + term[at, :].astype(f32)
            dst[at, :] = total.astype(dst.dtype)

    def add_relayed(t):
        ys = source(t)
        for step in range(NZ):
            arrived("er", t * 4 + step, R.rows_in.at[0])
            for way, goes in enumerate(ways):
                ref = R.relay.at[ys, way, step]
                add(ref, (ref, half_of(R.part.at[ys, cell(goes, order[step])], way)), SLOTS // 2)
                start("ev", t * 4 + step, ref, half_of(R.from_x.at[ys, way, step], way), {"x": goes})

    def x_terms(ys, step):
        own = R.part.at[ys, cell(x, order[step])]
        return [own, R.from_x.at[ys, 0, step], R.from_x.at[ys, 1, step]]

    def add_x(t):
        ys = source(t)
        arrived("eu", t, R.from_x.at[ys, 0])
        for step in range(NZ):
            arrived("ev", t * 4 + step, R.rows_in.at[0])
            if step < NZ - 1:
                mine = R.mine.at[ys, step]
                add(mine, x_terms(ys, step), SLOTS)
                start("eq", t, mine, R.from_z.at[ys, step], {"z": order[step]})

    def add_z(t):
        ys = source(t)
        arrived("eq", t, R.from_z.at[ys])
        terms = x_terms(ys, NZ - 1) + [R.from_z.at[ys, i] for i in range(NZ - 1)]

        @pl.when(t == 0)
        def _():
            add(R.returned.at[own_expert], terms, SLOTS)

        @pl.when(t > 0)
        def _():
            add(R.done.at[ys], terms, SLOTS)
            dy, dw = ahead(t)
            ty, tw = place(t)
            start("rt", 0, R.done.at[ys], R.returned.at[own_expert], {"y": ty, "w": tw})

    R.rows_in[own_expert] = place_rows(own_expert)
    begin(0)
    dispatch(1)
    dispatch(2)
    dispatch(3)
    begin(1)

    @pl.loop(0, STEPS + 5)
    def _(t):
        def stage(offset, what):
            @pl.when((t >= offset) & (t - offset < STEPS))
            def _():
                what(t - offset)

        stage(0, along_x)

        @pl.when(t + 4 < STEPS)
        def _():
            dispatch(t + 4)

        @pl.when(t + 2 < STEPS)
        def _():
            begin(t + 2)

        stage(1, pass_on)
        stage(4, add_x)
        stage(5, add_z)

        @pl.when(t == 2)
        def _():
            for i, (src, dst) in enumerate(taken):
                loads[i].wait()
                arrived(("twg", "twu", "twd")[i], 0, dst)

        def first(c):
            complete(c)
            hidden(c)

        stage(2, first)
        stage(3, add_relayed)
        stage(2, hand_out)

    arrived("rt", 0, R.returned.at[pl.ds(0, EXPERTS - 1)])
    results = R.returned[...].reshape(EXPERTS * SLOTS, WIDE)
    share = jnp.dot(R.picker[0], results, preferred_element_type=f32)
    share = share + jnp.dot(R.picker[1], results, preferred_element_type=f32)
    zero = jnp.zeros((TOK, WIDE), f32)
    parts = []
    for i in range(2):
        mine = R.stream[i * TOK : (i + 1) * TOK, :]
        parts += [jnp.where(k == 0, mine, zero), jnp.where(k == 0, zero, mine)]
    share = share + jnp.concatenate(parts, axis=0)
    first, second = share[:, :FEATS], share[:, FEATS:]
    R.give[...] = jnp.where(k == 0, second, first)
    start("ge", 0, R.give, R.got, {"k": 1 - k})
    keep = jnp.where(k == 0, first, second)
    arrived("ge", 0, R.got)
    mixed_ref[...] = (keep + R.got[...]).T.astype(bf16)

    for kind, many in (("kz", 3), ("kx", 8), ("kf", 4), ("kk", 12), ("kh", 4)):
        left(kind, held.at[pl.ds(0, many)])
    for kind, many in (("az", 3), ("ax", 8), ("af", 4)):
        left(kind, slab.at[pl.ds(0, many * TOK)])
    left("ap", R.pieces.at[pl.ds(0, EXPERTS - 1)])
    left("ab", R.both.at[pl.ds(0, 2 * TOK)])
    left("dd", R.rows_in.at[pl.ds(0, EXPERTS - 1)])
    left("rt", R.rows_in.at[pl.ds(0, EXPERTS - 1)])
    left("ge", R.give)
    left("two", R.wo.at[feats_of(0)])
    left("tre", R.res.at[feats_of(0)])
    for i, (src, dst) in enumerate(taken):
        left(("twg", "twu", "twd")[i], dst)
    left("ez", R.from_z)
    left("eq", R.from_z)
    left("ex", R.from_x)
    for kind in ("ef", "er", "eu", "ev"):
        left(kind, R.relay)


def local(
    queries,
    rotated_key_cache,
    value_cache_rows,
    kv_pos,
    q_pos,
    residual,
    w_out,
    norm_gain,
    routes,
    gate_probs,
    w_gate,
    w_up,
    w_down,
):
    any_spec, vmem_spec = pl.BlockSpec(memory_space=pl.ANY), pl.BlockSpec(memory_space=pltpu.VMEM)
    flops = 2 * STEPS * SLOTS * D * HID * 3
    attended, mixed = pl.pallas_call(
        layer_kernel,
        out_shape=(
            jax.ShapeDtypeStruct((TOK, JOINED), bf16),
            jax.ShapeDtypeStruct((FEATS, BLOCK), bf16),
        ),
        in_specs=[vmem_spec] * 7 + [any_spec] + [vmem_spec] * 2 + [any_spec] * 3,
        out_specs=(vmem_spec, vmem_spec),
        scratch_shapes=list(SCRATCH.values()),
        compiler_params=pltpu.CompilerParams(
            collective_id=1, has_side_effects=True, vmem_limit_bytes=63 << 20
        ),
        cost_estimate=pl.CostEstimate(flops=flops, bytes_accessed=20 << 20, transcendentals=0),
        name="layer",
    )(
        queries,
        q_pos[None, :],
        rotated_key_cache,
        value_cache_rows,
        kv_pos.reshape(2, 128),
        norm_gain[None, :],
        residual.T,
        w_out.T,
        routes.T,
        gate_probs.T,
        w_gate[0],
        w_up[0],
        w_down[0],
    )
    return attended, mixed.T


def solution(mesh):
    fine = Mesh(mesh.devices.reshape(NX, NZ, 2, 4, 2), ("x", "z", "k", "y", "w"))
    ctx, exp = ("x", "z", "k"), ("y", "w")
    in_specs = (
        P(ctx, exp),
        P(ctx, exp),
        P(ctx, exp),
        P(ctx),
        P(ctx),
        P(exp, ctx),
        P(exp, ctx),
        P(ctx),
        P(exp, None),
        P(exp, None),
        P(exp, None, ctx),
        P(exp, None, ctx),
        P(exp, ctx, None),
    )
    out_specs = (P(ctx, exp), P(exp, ctx))
    return jax.shard_map(local, mesh=fine, in_specs=in_specs, out_specs=out_specs, check_vma=False)
```

```python
import jax
import jax.numpy as jnp
from jax import lax
from jax.experimental import pallas as pl
from jax.experimental.pallas import tpu as pltpu
from jax.sharding import Mesh
from jax.sharding import PartitionSpec as P

MESH = pl.DeviceIdType.MESH
DMA = pltpu.SemaphoreType.DMA
D = 6144
NX, NZ, NY = 4, 4, 4
STEPS = 8
EXPERTS = 8
neg_big = -1e30
epsilon = 1e-05
LOG2E = 1.4426950408889634

TOK, HEAD, HEADS, POS, BLOCK, SLOTS, WIDE, HID = 64, 128, 6, 256, 256, 96, 384, 512
JOINED = HEADS * HEAD
FEATS = WIDE // 2
DEEP = POS + 16

bf16, f32 = jnp.bfloat16, jnp.float32


def vmem(*shape, kind=bf16):
    return pltpu.VMEM(shape, kind)


SCRATCH = {
    "held": vmem(2 * NX * NZ, DEEP, 2 * HEAD),
    "q_rows": vmem(TOK * HEADS, HEAD),
    "limit": vmem(2 * TOK, 1, kind=f32),
    "top": vmem(TOK * HEADS, HEAD, kind=f32),
    "acc": vmem(TOK * HEADS, 2 * HEAD, kind=f32),
    "gain_squares": vmem(NX * NZ, 1, WIDE, kind=f32),
    "slab": vmem(NX * NZ * TOK, JOINED),
    "wo": vmem(WIDE, JOINED),
    "res": vmem(WIDE, BLOCK),
    "res_rows": vmem(BLOCK, WIDE),
    "leaving": vmem(NX, NZ * TOK, WIDE),
    "pieces": vmem(EXPERTS, 2 * TOK, WIDE),
    "stream": vmem(2 * TOK, WIDE, kind=f32),
    "both": vmem(BLOCK, WIDE),
    "placer": vmem(EXPERTS * SLOTS, BLOCK),
    "picker": vmem(2, BLOCK, EXPERTS * SLOTS),
    "rows_out": vmem(EXPERTS, SLOTS, WIDE),
    "rows_in": vmem(STEPS, SLOTS, WIDE),
    "spread": vmem(STEPS, NX * NZ, SLOTS, WIDE),
    "part": vmem(STEPS, NX * NZ, SLOTS, WIDE),
    "relay": vmem(STEPS, 2, NZ, SLOTS // 2, WIDE),
    "from_x": vmem(STEPS, 2, NZ, SLOTS, WIDE),
    "mine": vmem(STEPS, NZ - 1, SLOTS, WIDE),
    "from_z": vmem(STEPS, NZ - 1, SLOTS, WIDE),
    "done": vmem(STEPS, SLOTS, WIDE),
    "wg": vmem(D, HID),
    "wu": vmem(D, HID),
    "wd": vmem(HID, D),
    "gate_sum": vmem(SLOTS, HID, kind=f32),
    "up_sum": vmem(SLOTS, HID, kind=f32),
    "squares": vmem(SLOTS, 128, kind=f32),
    "act": vmem(SLOTS, HID),
    "returned": vmem(EXPERTS, SLOTS, WIDE),
    "give": vmem(BLOCK, FEATS, kind=f32),
    "got": vmem(BLOCK, FEATS, kind=f32),
    "w_sem": DMA((4,)),
    "own_sem": DMA((STEPS,)),
}
KINDS = {
    "kz": 6, "kx": 8, "kf": 4, "kk": 8, "kh": 4,
    "az": 6, "ax": 8, "af": 1, "ap": 1, "ab": 1,
    "dd": 8, "rt": 1, "ge": 1, "two": 1, "tre": 1, "twg": 1, "twu": 1, "twd": 1,
    "ez": 3 * STEPS, "ex": 4 * STEPS, "ef": STEPS,
    "er": 4 * STEPS, "eu": STEPS, "ev": 4 * STEPS, "eq": STEPS,
}
SCRATCH["sent"] = DMA((len(KINDS),))
for kind, many in KINDS.items():
    SCRATCH[kind] = DMA((many,))


def remote(src, dst, send_sem, recv_sem, device):
    return pltpu.make_async_remote_copy(
        src_ref=src,
        dst_ref=dst,
        send_sem=send_sem,
        recv_sem=recv_sem,
        device_id=device,
        device_id_type=MESH,
    )


def layer_kernel(
    q_ref, q_pos_ref, k_ref, v_ref, page_ref, gain_ref, res_ref, wo_ref, routes_ref, probs_ref,
    wg_ref, wu_ref, wd_ref, att_ref, mixed_ref, *refs,
):
    at_name = dict(zip(SCRATCH, refs))

    class R:
        pass

    for name, ref in at_name.items():
        setattr(R, name, ref)
    x, z, k, y, w = (lax.axis_index(name) for name in ("x", "z", "k", "y", "w"))
    up, down, across = lax.rem(x + 1, NX), lax.rem(x + 3, NX), lax.rem(x + 2, NX)
    ways = (up, down)
    order = [lax.rem(z + step, NZ) for step in (1, 2, 3, 0)]
    others = [(dy, dw) for dy in range(NY) for dw in range(2) if (dy, dw) != (0, 0)]
    own_expert = 2 * y + w

    kinds = list(KINDS)

    def start(kind, at, src, dst, device):
        remote(src, dst, R.sent.at[kinds.index(kind)], at_name[kind].at[at], device).start()

    def arrived(kind, at, ref):
        remote(ref, ref, R.sent.at[kinds.index(kind)], at_name[kind].at[at], {"x": up}).wait_recv()

    def left(kind, ref):
        remote(ref, ref, R.sent.at[kinds.index(kind)], at_name[kind].at[0], {"x": up}).wait_send()

    def behind(step):
        return lax.rem(z + NZ - step, NZ)

    held = R.held
    own = 2 * (x * NZ + z) + k
    held[own, :POS, :HEAD] = k_ref[...]
    held[own, :POS, HEAD:] = v_ref[...]
    pages = page_ref[...].astype(f32) * (1.0 / 128.0)
    row = lax.broadcasted_iota(jnp.int32, (16, 2 * HEAD), 0)
    lane = lax.broadcasted_iota(jnp.int32, (16, 2 * HEAD), 1)
    numbers = jnp.where(lane == 0, pages[0:1, 0:1], jnp.where(lane == 1, pages[1:2, 0:1], 0.0))
    gain = jnp.concatenate([gain_ref[...].astype(f32), jnp.zeros((1, 2 * HEAD - FEATS), f32)], axis=1)
    extra = jnp.where(row == 0, numbers, jnp.where(row == 1, gain, 0.0))
    held[own, POS:, :] = extra.astype(bf16)

    barrier = pltpu.get_barrier_semaphore()
    peers = [{"x": up}, {"x": down}, {"k": 1 - k}]
    peers += [{"z": lax.rem(z + step, NZ)} for step in range(1, NZ)]
    peers += [{"y": lax.rem(y + dy, NY), "w": lax.rem(w + dw, 2)} for dy, dw in others]
    for device in peers:
        pl.semaphore_signal(barrier, inc=1, device_id=device, device_id_type=MESH)
    pl.semaphore_wait(barrier, len(peers))

    halves = ((0, 144), (144, DEEP - 144))

    def spot(bx, bz, core, half=None):
        where = 2 * (bx * NZ + bz) + core
        if half is None:
            return held.at[where]
        return held.at[where, pl.ds(*halves[half])]

    block = spot(x, z, k)
    for part in range(2):
        piece = spot(x, z, k, part)
        for step in range(1, NZ):
            start("kz", 2 * (step - 1) + part, piece, piece, {"z": lax.rem(z + step, NZ)})
        for goes in ways:
            start("kx", part, piece, piece, {"x": goes})
    start("kk", 0, block, block, {"k": 1 - k})

    def feats_of(core):
        return pl.ds(pl.multiple_of(core * FEATS, 16), FEATS)

    local_wo = pltpu.make_async_copy(wo_ref, R.wo.at[feats_of(k)], R.w_sem.at[0])
    local_wo.start()
    start("two", 0, wo_ref, R.wo.at[feats_of(k)], {"k": 1 - k})
    R.res[feats_of(k), :] = res_ref[...]
    start("tre", 0, res_ref, R.res.at[feats_of(k)], {"k": 1 - k})

    def upright(rows):
        return jnp.concatenate([rows.astype(f32), jnp.zeros((6, BLOCK), f32)], axis=0).T

    routes = upright(routes_ref[...]).astype(jnp.int32)
    probs = upright(probs_ref[...])
    expert_lane = lax.broadcasted_iota(jnp.int32, (BLOCK, 128), 1)
    named = [(routes[:, c : c + 1] == expert_lane).astype(f32) for c in range(2)]
    before = lax.broadcasted_iota(jnp.int32, (BLOCK, BLOCK), 0) > lax.broadcasted_iota(
        jnp.int32, (BLOCK, BLOCK), 1
    )
    earlier = jnp.dot(
        before.astype(f32).astype(bf16), (named[0] + named[1]).astype(bf16), preferred_element_type=f32
    )
    slot_lane = lax.broadcasted_iota(jnp.int32, (BLOCK, EXPERTS * SLOTS), 1)
    hits = []
    for c in range(2):
        slot = jnp.sum(earlier * named[c], axis=1, keepdims=True).astype(jnp.int32) - k * SLOTS
        ok = (slot >= 0) & (slot < SLOTS)
        hits.append(jnp.where(ok, routes[:, c : c + 1] * SLOTS + slot, -1) == slot_lane)
    placer = jnp.where(hits[0], 1.0, jnp.where(hits[1], 1.0, 0.0))
    R.placer[...] = placer.T.astype(bf16)
    picker = jnp.where(hits[0], probs[:, 0:1], jnp.where(hits[1], probs[:, 1:2], 0.0))
    high = picker.astype(bf16)
    R.picker[0] = high
    R.picker[1] = (picker - high.astype(f32)).astype(bf16)

    for h in range(HEADS):
        R.q_rows[pl.ds(h * TOK, TOK), :] = q_ref[:, pl.ds(h * HEAD, HEAD)]
    R.top[...] = jnp.full_like(R.top, neg_big)
    R.acc[...] = jnp.zeros_like(R.acc)
    limit = jnp.broadcast_to(q_pos_ref[...].astype(f32), (8, TOK)).T[:, 0:1]
    R.limit[...] = jnp.concatenate([limit, limit], axis=0)
    scaling = HEAD**-0.5 * LOG2E
    tile = 2 * TOK

    def attend(bx, bz):
        where = 2 * (bx * NZ + bz)
        terms = []
        steps = lax.broadcasted_iota(jnp.int32, (1, HEAD), 1).astype(f32)
        for core in range(2):
            starts = held[where + core, POS:, :HEAD].astype(f32)
            positions = jnp.concatenate(
                [starts[0:1, 0:1] * 128.0 + steps, starts[0:1, 1:2] * 128.0 + steps], axis=1
            )
            terms.append((held[where + core, :POS, :HEAD], held[where + core, :POS, HEAD:], positions))
        ones = jnp.ones((POS, HEAD), bf16)
        limit = R.limit[...]
        for r in range(TOK * HEADS // tile):
            at = pl.ds(r * tile, tile)
            scores = []
            for keys, _, positions in terms:
                score = lax.dot_general(
                    R.q_rows[at, :], keys, (((1,), (1,)), ((), ())), preferred_element_type=f32
                )
                scores.append(jnp.where(positions <= limit, score * scaling, neg_big))
            most = jnp.maximum(scores[0], scores[1])
            most = jnp.max(jnp.maximum(most[:, :HEAD], most[:, HEAD:]), axis=1, keepdims=True)
            old = R.top[at, :]
            new = jnp.maximum(old, most)
            R.top[at, :] = new
            fade = jnp.exp2(old - new)
            total = R.acc[at, :] * jnp.concatenate([fade, fade], axis=1)
            new = jnp.concatenate([new, new], axis=1)
            for score, (_, values, _) in zip(scores, terms):
                weights = jnp.exp2(score - new).astype(bf16)
                total = total + jnp.dot(
                    weights, jnp.concatenate([values, ones], axis=1), preferred_element_type=f32
                )
            R.acc[at, :] = total

    arrived("kk", 0, spot(x, z, 1 - k))
    attend(x, z)

    for part in range(2):
        for step in range(1, NZ):
            piece = spot(x, behind(step), k, part)
            arrived("kz", 2 * (step - 1) + part, piece)
            for goes in ways:
                start("kx", 2 * step + part, piece, piece, {"x": goes})
            if part == 1:
                ref = spot(x, behind(step), k)
                start("kk", step, ref, ref, {"k": 1 - k})

    @pl.loop(0, NZ)
    def _(step):
        bz = behind(step)
        for way, (came, goes) in enumerate(((down, up), (up, down))):
            arrived("kx", 2 * step + way, held.at[pl.ds(0, 2), pl.ds(*halves[way])])
            half = spot(came, bz, k, way)
            start("kf", step, half, half, {"x": goes})
        for came in (down, up):
            ref = spot(came, bz, k)
            start("kk", NZ + step, ref, ref, {"k": 1 - k})

        @pl.when(step > 0)
        def _():
            arrived("kk", step, spot(x, bz, 1 - k))
            attend(x, bz)

    @pl.loop(0, NZ)
    def _(step):
        bz = behind(step)
        ref = spot(across, bz, k)
        arrived("kf", step, ref)
        start("kh", step, ref, ref, {"k": 1 - k})
        arrived("kk", NZ + step, held.at[pl.ds(0, 2)])
        for came in (down, up):
            attend(came, bz)

    loads = [
        pltpu.make_async_copy(src, dst, R.w_sem.at[1 + i])
        for i, (src, dst) in enumerate(
            (
                (wg_ref, R.wg.at[:, pl.ds(0, HID // 2)]),
                (wu_ref, R.wu.at[:, pl.ds(0, HID // 2)]),
                (wd_ref, R.wd.at[pl.ds(0, HID // 2)]),
            )
        )
    ]
    taken = (
        (wg_ref, R.wg.at[:, pl.ds(HID // 2, HID // 2)]),
        (wu_ref, R.wu.at[:, pl.ds(HID // 2, HID // 2)]),
        (wd_ref, R.wd.at[pl.ds(HID // 2, HID // 2)]),
    )

    @pl.loop(0, NZ)
    def _(step):
        bz = behind(step)
        arrived("kh", step, spot(across, bz, 1 - k))
        attend(across, bz)

    for i, (src, dst) in enumerate(taken):
        loads[i].start()
        start(("twg", "twu", "twd")[i], 0, src, dst, {"k": 1 - k})

    slab = R.slab

    def strip(bx, bz, way=None):
        first = pl.multiple_of((bx * NZ + bz) * TOK, 16)
        if way is None:
            return slab.at[pl.ds(first, TOK)]
        return slab.at[pl.ds(pl.multiple_of(first + way * (TOK // 2), 16), TOK // 2)]

    for h in range(HEADS):
        at = pl.ds(h * TOK, TOK)
        att_ref[:, pl.ds(h * HEAD, HEAD)] = (R.acc[at, :HEAD] / R.acc[at, HEAD:]).astype(bf16)
    slab[pl.ds(pl.multiple_of((x * NZ + z) * TOK, 16), TOK), :] = att_ref[...]
    rows = strip(x, z)
    for part in range(2):
        piece = strip(x, z, part)
        for step in range(1, NZ):
            start("az", 2 * (step - 1) + part, piece, piece, {"z": lax.rem(z + step, NZ)})
        for goes in ways:
            start("ax", part, piece, piece, {"x": goes})

    for b in range(NX * NZ):
        pair = [held[2 * b + core, POS:, :].astype(f32)[1:2, :FEATS] for core in range(2)]
        gains = jnp.concatenate(pair, axis=1)
        R.gain_squares[b] = 1.0 / (gains * gains)
    local_wo.wait()
    arrived("two", 0, R.wo.at[feats_of(1 - k)])
    arrived("tre", 0, R.res.at[feats_of(1 - k)])
    R.res_rows[...] = R.res[...].astype(f32).T.astype(bf16)

    for part in range(2):
        for step in range(1, NZ):
            piece = strip(x, behind(step), part)
            arrived("az", 2 * (step - 1) + part, piece)
            for goes in ways:
                start("ax", 2 * step + part, piece, piece, {"x": goes})

    def project_rows(bx):
        at = pl.ds(pl.multiple_of(bx * (NZ * TOK), 16), NZ * TOK)
        R.leaving[bx] = lax.dot_general(
            slab[at, :], R.wo[...], (((1,), (1,)), ((), ())), preferred_element_type=f32
        ).astype(bf16)
        for tw in range(2):
            here = (bx == y) & (tw == w)

            @pl.when(here)
            def _():
                R.pieces[own_expert] = R.leaving[bx, tw * 2 * TOK : (tw + 1) * 2 * TOK, :]

            @pl.when(jnp.logical_not(here))
            def _():
                piece = R.leaving.at[bx, pl.ds(tw * 2 * TOK, 2 * TOK)]
                start("ap", 0, piece, R.pieces.at[own_expert], {"y": bx, "w": tw})

    project_rows(x)
    for step in range(NZ):
        bz = behind(step)
        for way, (came, goes) in enumerate(((down, up), (up, down))):
            arrived("ax", 2 * step + way, slab.at[pl.ds(0, TOK)])
            ref = strip(came, bz, way)
            start("af", 0, ref, ref, {"x": goes})
    project_rows(up)
    project_rows(down)
    arrived("af", 0, slab.at[pl.ds(0, NZ * TOK)])
    project_rows(across)

    def token_rows(core, i):
        return pl.ds(pl.multiple_of(2 * TOK * i + core * TOK, 16), TOK)

    arrived("ap", 0, R.pieces.at[pl.ds(0, EXPERTS - 1)])
    total = jnp.concatenate([R.res_rows[token_rows(k, i), :] for i in range(2)], axis=0).astype(f32)
    for i in range(EXPERTS):
        total = total + R.pieces[i].astype(f32)
    R.stream[...] = total
    gain_pair = [
        held[2 * (x * NZ + z) + core, POS:, :].astype(f32)[1:2, :FEATS] for core in range(2)
    ]
    scaled = (total * jnp.concatenate(gain_pair, axis=1)).astype(bf16)

    for i in range(2):
        R.both[token_rows(k, i), :] = scaled[i * TOK : (i + 1) * TOK, :]
        ref = R.both.at[token_rows(k, i)]
        start("ab", 0, ref, ref, {"k": 1 - k})
    arrived("ab", 0, R.both.at[pl.ds(0, 2 * TOK)])

    def ahead(t):
        return lax.rem(t, 2) + 2 * (t // 4), lax.rem((t + 2) // 4, 2)

    def place(t):
        dy, dw = ahead(t)
        return lax.rem(y + dy, NY), lax.rem(w + dw, 2)

    def source(t):
        sy, sw = place(t)
        return 2 * sy + sw

    def place_rows(expert):
        at = pl.ds(pl.multiple_of(expert * SLOTS, 16), SLOTS)
        return jnp.dot(R.placer[at, :], R.both[...], preferred_element_type=f32).astype(bf16)

    def dispatch(t):
        dy, dw = ahead(t)
        dy = lax.rem(NY - dy, NY)
        ty, tw = lax.rem(y + dy, NY), lax.rem(w + dw, 2)
        e = 2 * ty + tw
        R.rows_out[e] = place_rows(e)
        start("dd", 2 * dy + dw, R.rows_out.at[e], R.rows_in.at[own_expert], {"y": ty, "w": tw})

    def cell(bx, bz):
        return bx * NZ + bz

    def half_of(ref, way):
        return ref.at[pl.ds(way * (SLOTS // 2), SLOTS // 2)]

    def keep_own(t):
        ys = source(t)
        return pltpu.make_async_copy(R.rows_in.at[ys], R.spread.at[ys, x * NZ + z], R.own_sem.at[t])

    def begin(t):
        ys = source(t)
        dy, dw = ahead(t)
        j = 2 * lax.rem(NY - dy, NY) + dw

        @pl.when(t > 0)
        def _():
            arrived("dd", j, R.rows_in.at[ys])

        keep_own(t).start()
        src, dst = R.rows_in.at[ys], R.spread.at[ys, x * NZ + z]
        for step in range(1, NZ):
            start("ez", t * 3 + step - 1, src, dst, {"z": lax.rem(z + step, NZ)})
        for way, goes in enumerate(ways):
            start("ex", t * 4, src, dst, {"x": goes})

    def along_x(t):
        ys = source(t)
        for step in range(1, NZ):
            ref = R.spread.at[ys, cell(x, behind(step))]
            arrived("ez", t * 3 + step - 1, ref)
            for way, goes in enumerate(ways):
                start("ex", t * 4 + step, ref, ref, {"x": goes})

    def pass_on(t):
        ys = source(t)
        for step in range(NZ):
            arrived("ex", t * 4 + step, R.from_x.at[ys, 0, pl.ds(0, 2)])
            for way, (came, goes) in enumerate(((down, up), (up, down))):
                ref = half_of(R.spread.at[ys, cell(came, behind(step))], way)
                start("ef", t, ref, ref, {"x": goes})

    def complete(t):
        ys = source(t)
        arrived("ef", t, R.spread.at[ys, pl.ds(across * NZ, NZ)])
        keep_own(t).wait()

    deep = 2 * WIDE

    def hidden(t):
        ys = source(t)
        R.gate_sum[...] = jnp.zeros_like(R.gate_sum)
        R.up_sum[...] = jnp.zeros_like(R.up_sum)
        R.squares[...] = jnp.zeros_like(R.squares)

        @pl.loop(0, D // deep)
        def _(i):
            at = pl.ds(pl.multiple_of(i * deep, 128), deep)
            piece = jnp.concatenate([R.spread[ys, 2 * i], R.spread[ys, 2 * i + 1]], axis=1)
            R.gate_sum[...] += jnp.dot(piece, R.wg[at, :], preferred_element_type=f32)
            R.up_sum[...] += jnp.dot(piece, R.wu[at, :], preferred_element_type=f32)
            wide = piece.astype(f32)
            wide = wide * wide
            wide = wide * jnp.concatenate([R.gain_squares[2 * i], R.gain_squares[2 * i + 1]], axis=1)
            total = wide[:, :128]
            for lane in range(128, deep, 128):
                total = total + wide[:, lane : lane + 128]
            R.squares[...] += total

        tile = 48

        @pl.loop(0, SLOTS // tile)
        def _(i):
            at = pl.ds(i * tile, tile)
            inverse = lax.rsqrt(jnp.sum(R.squares[at, :], axis=1, keepdims=True) / D + epsilon)
            gate = R.gate_sum[at, :] * inverse
            R.act[at, :] = (gate / (1.0 + jnp.exp(-gate)) * (R.up_sum[at, :] * inverse)).astype(bf16)

    def project(t, bx):
        ys = source(t)
        for i in range(NZ // 2):
            at = pl.ds(pl.multiple_of(bx * (NZ * WIDE) + i * deep, 128), deep)
            term = jnp.dot(R.act[...], R.wd[:, at], preferred_element_type=f32).astype(bf16)
            R.part[ys, cell(bx, 2 * i)] = term[:, :WIDE]
            R.part[ys, cell(bx, 2 * i + 1)] = term[:, WIDE:]

    def hand_out(t):
        ys = source(t)
        project(t, across)
        for step in range(NZ):
            for way, goes in enumerate(ways):
                ref = half_of(R.part.at[ys, cell(across, order[step])], way)
                start("er", t * 4 + step, ref, R.relay.at[ys, way, step], {"x": goes})
        for way, goes in enumerate(ways):
            project(t, goes)
            for step in range(NZ):
                ref = half_of(R.part.at[ys, cell(goes, order[step])], 1 - way)
                dst = half_of(R.from_x.at[ys, way, step], 1 - way)
                start("eu", t, ref, dst, {"x": goes})
        project(t, x)

    def add(dst, terms, count):
        tile = 48

        @pl.loop(0, count // tile)
        def _(i):
            at = pl.ds(i * tile, tile)
            total = terms[0][at, :].astype(f32)
            for term in terms[1:]:
                total = total + term[at, :].astype(f32)
            dst[at, :] = total.astype(dst.dtype)

    def add_relayed(t):
        ys = source(t)
        for step in range(NZ):
            arrived("er", t * 4 + step, R.rows_in.at[0])
            for way, goes in enumerate(ways):
                ref = R.relay.at[ys, way, step]
                add(ref, (ref, half_of(R.part.at[ys, cell(goes, order[step])], way)), SLOTS // 2)
                start("ev", t * 4 + step, ref, half_of(R.from_x.at[ys, way, step], way), {"x": goes})

    def x_terms(ys, step):
        own = R.part.at[ys, cell(x, order[step])]
        return [own, R.from_x.at[ys, 0, step], R.from_x.at[ys, 1, step]]

    def add_x(t):
        ys = source(t)
        arrived("eu", t, R.from_x.at[ys, 0])
        for step in range(NZ):
            arrived("ev", t * 4 + step, R.rows_in.at[0])
            if step < NZ - 1:
                mine = R.mine.at[ys, step]
                add(mine, x_terms(ys, step), SLOTS)
                start("eq", t, mine, R.from_z.at[ys, step], {"z": order[step]})

    def add_z(t):
        ys = source(t)
        arrived("eq", t, R.from_z.at[ys])
        terms = x_terms(ys, NZ - 1) + [R.from_z.at[ys, i] for i in range(NZ - 1)]

        @pl.when(t == 0)
        def _():
            add(R.returned.at[own_expert], terms, SLOTS)

        @pl.when(t > 0)
        def _():
            add(R.done.at[ys], terms, SLOTS)
            dy, dw = ahead(t)
            ty, tw = place(t)
            start("rt", 0, R.done.at[ys], R.returned.at[own_expert], {"y": ty, "w": tw})

    R.rows_in[own_expert] = place_rows(own_expert)
    begin(0)
    dispatch(1)
    dispatch(2)
    dispatch(3)
    begin(1)
    dispatch(4)
    begin(2)

    @pl.loop(0, STEPS + 5)
    def _(t):
        def stage(offset, what):
            @pl.when((t >= offset) & (t - offset < STEPS))
            def _():
                what(t - offset)

        stage(1, pass_on)

        @pl.when(t + 5 < STEPS)
        def _():
            dispatch(t + 5)

        @pl.when(t + 3 < STEPS)
        def _():
            begin(t + 3)

        stage(0, along_x)
        stage(4, add_x)
        stage(5, add_z)

        @pl.when(t == 2)
        def _():
            for i, (src, dst) in enumerate(taken):
                loads[i].wait()
                arrived(("twg", "twu", "twd")[i], 0, dst)

        def first(c):
            complete(c)
            hidden(c)

        stage(2, first)
        stage(3, add_relayed)
        stage(2, hand_out)

    arrived("rt", 0, R.returned.at[pl.ds(0, EXPERTS - 1)])
    results = R.returned[...].reshape(EXPERTS * SLOTS, WIDE)
    share = jnp.dot(R.picker[0], results, preferred_element_type=f32)
    share = share + jnp.dot(R.picker[1], results, preferred_element_type=f32)
    zero = jnp.zeros((TOK, WIDE), f32)
    parts = []
    for i in range(2):
        mine = R.stream[i * TOK : (i + 1) * TOK, :]
        parts += [jnp.where(k == 0, mine, zero), jnp.where(k == 0, zero, mine)]
    share = share + jnp.concatenate(parts, axis=0)
    first, second = share[:, :FEATS], share[:, FEATS:]
    R.give[...] = jnp.where(k == 0, second, first)
    start("ge", 0, R.give, R.got, {"k": 1 - k})
    keep = jnp.where(k == 0, first, second)
    arrived("ge", 0, R.got)
    mixed_ref[...] = (keep + R.got[...]).T.astype(bf16)

    for kind, many in (("kz", 3), ("kx", 8), ("kf", 4), ("kk", 12), ("kh", 4)):
        left(kind, held.at[pl.ds(0, many)])
    for kind, many in (("az", 3), ("ax", 8), ("af", 4)):
        left(kind, slab.at[pl.ds(0, many * TOK)])
    left("ap", R.pieces.at[pl.ds(0, EXPERTS - 1)])
    left("ab", R.both.at[pl.ds(0, 2 * TOK)])
    left("dd", R.rows_in.at[pl.ds(0, EXPERTS - 1)])
    left("rt", R.rows_in.at[pl.ds(0, EXPERTS - 1)])
    left("ge", R.give)
    left("two", R.wo.at[feats_of(0)])
    left("tre", R.res.at[feats_of(0)])
    for i, (src, dst) in enumerate(taken):
        left(("twg", "twu", "twd")[i], dst)
    left("ez", R.from_z)
    left("eq", R.from_z)
    left("ex", R.from_x)
    for kind in ("ef", "er", "eu", "ev"):
        left(kind, R.relay)


def local(
    queries,
    rotated_key_cache,
    value_cache_rows,
    kv_pos,
    q_pos,
    residual,
    w_out,
    norm_gain,
    routes,
    gate_probs,
    w_gate,
    w_up,
    w_down,
):
    any_spec, vmem_spec = pl.BlockSpec(memory_space=pl.ANY), pl.BlockSpec(memory_space=pltpu.VMEM)
    flops = 2 * STEPS * SLOTS * D * HID * 3
    attended, mixed = pl.pallas_call(
        layer_kernel,
        out_shape=(
            jax.ShapeDtypeStruct((TOK, JOINED), bf16),
            jax.ShapeDtypeStruct((FEATS, BLOCK), bf16),
        ),
        in_specs=[vmem_spec] * 7 + [any_spec] + [vmem_spec] * 2 + [any_spec] * 3,
        out_specs=(vmem_spec, vmem_spec),
        scratch_shapes=list(SCRATCH.values()),
        compiler_params=pltpu.CompilerParams(
            collective_id=1, has_side_effects=True, vmem_limit_bytes=63 << 20
        ),
        cost_estimate=pl.CostEstimate(flops=flops, bytes_accessed=20 << 20, transcendentals=0),
        name="layer",
    )(
        queries,
        q_pos[None, :],
        rotated_key_cache,
        value_cache_rows,
        kv_pos.reshape(2, 128),
        norm_gain[None, :],
        residual.T,
        w_out.T,
        routes.T,
        gate_probs.T,
        w_gate[0],
        w_up[0],
        w_down[0],
    )
    return attended, mixed.T


def solution(mesh):
    fine = Mesh(mesh.devices.reshape(NX, NZ, 2, 4, 2), ("x", "z", "k", "y", "w"))
    ctx, exp = ("x", "z", "k"), ("y", "w")
    in_specs = (
        P(ctx, exp),
        P(ctx, exp),
        P(ctx, exp),
        P(ctx),
        P(ctx),
        P(exp, ctx),
        P(exp, ctx),
        P(ctx),
        P(exp, None),
        P(exp, None),
        P(exp, None, ctx),
        P(exp, None, ctx),
        P(exp, ctx, None),
    )
    out_specs = (P(ctx, exp), P(exp, ctx))
    return jax.shard_map(local, mesh=fine, in_specs=in_specs, out_specs=out_specs, check_vma=False)
```
